256 devices in a mesh: dp: 4 (over x), ctx: 64 (over z, y, core).
Axes of the slice: x: 4, y: 4, z: 8, core: 2. Of those that a mesh axis runs over, the one named last changes fastest.
Arguments:
- queries: bfloat16 [32768, 1024], P(('dp', 'ctx')), parts along dimension 0, may hold values from -6 to 6
- keys: bfloat16 [32768, 1024], P(('dp', 'ctx')), parts along dimension 0, may hold values from -6 to 6
- values: bfloat16 [32768, 1024], P(('dp', 'ctx')), parts along dimension 0, may hold values from -6 to 6
- out_grad: bfloat16 [32768, 1024], P(('dp', 'ctx')), parts along dimension 0, may hold values from -6 to 6
- offsets: int32 [24, 8], P('dp'), parts along dimension 0, may hold values from 0 to 31, as said below
Outputs:
- attended: bfloat16 [32768, 1024], P(('dp', 'ctx')), parts along dimension 0
- query_grad: bfloat16 [32768, 1024], P(('dp', 'ctx')), parts along dimension 0
- key_grad: bfloat16 [32768, 1024], P(('dp', 'ctx')), parts along dimension 0
- value_grad: bfloat16 [32768, 1024], P(('dp', 'ctx')), parts along dimension 0
The draws below stay inside these ranges and needn't reach their ends.
There are 4 independent parts, one for each index of `dp`. The reference program is written for one: setup_inputs(seed, part) draws one part's arguments, and reference() takes and returns one part's arrays. A program takes and returns all parts, laid end to end along the dimension named above; each array names one. Nothing has to cross between parts.
Inputs may be any that keep to these rules, and one draw needn't show every extreme that they name: offsets[l, h] is below 2^l and equals offsets[5, h] modulo 2^l; the top level's offsets of the heads are distinct.
All inputs are finite; a program needn't handle non-finite values.
Results may differ from the reference program's by a relative error of at most 0.0049.
The reference program's roundings to bfloat16 on the way count: a program that leaves them out, or rounds other values in their place, can miss the bound.
Values may be sent and summed in bfloat16 or wider, within the bound.
No kernel may reach another device: no remote copies, remote signals or barrier semaphores. Data moves between devices by JAX's collectives and lax.ppermute only.
A program may use at most 128 MiB of HBM per device.

```python
import math
import jax
import jax.numpy as jnp
from jax import lax

HEADS = 8
HEAD_DIM = 128
LEVELS = 6
TOKENS = 8192
FEATURES = 1024


def head_bases(key):
    key = jax.random.fold_in(key, 11)
    order = jax.random.permutation(key, 2 ** (LEVELS - 1))
    chosen = order[:HEADS]
    return jnp.where(chosen == jnp.max(chosen), 2 ** (LEVELS - 1) - 1, chosen).astype(jnp.int32)


def draw_offsets(key, part):
    bases = head_bases(key)
    dilations = 2 ** jnp.arange(LEVELS, dtype=jnp.int32)
    return (bases[None, :] % dilations[:, None]).astype(jnp.int32)


def draw_queries(key, part):
    key = jax.random.fold_in(key, 3)
    drawn = 2.0 * jax.random.truncated_normal(key, -3.0, 3.0, (TOKENS, HEADS, HEAD_DIM), jnp.float32)
    return drawn.reshape(TOKENS, HEADS * HEAD_DIM).astype(jnp.bfloat16)


def draw_keys(key, part):
    key = jax.random.fold_in(key, 5)
    drawn = jax.random.truncated_normal(key, -6.0, 6.0, (TOKENS, HEADS, HEAD_DIM), jnp.float32)
    return drawn.reshape(TOKENS, HEADS * HEAD_DIM).astype(jnp.bfloat16)


def level_of(rng, shape, cuts, smallest, high):
    level = 1.0
    for dim, shards_of in cuts:
        heights = jax.random.uniform(jax.random.fold_in(jax.random.fold_in(rng, 6), dim), (shards_of,), jnp.float32, smallest / len(cuts), high / len(cuts))
        level = level * jnp.repeat(jnp.exp(heights), shape[dim] // shards_of).reshape((-1,) + (1,) * (len(shape) - 1 - dim))
    return level


def noise(stream_key, dims, scale, reach, cuts=(), held_as=jnp.bfloat16):
    values = jax.random.normal(stream_key, dims, jnp.float32) * scale
    if len(cuts) > 0:
        values = level_of(stream_key, dims, cuts, -0.22, 0.18) * values
    return jnp.clip(values, min=-reach, max=reach).astype(held_as)


def setup_inputs(seed: int = 0, part: int = 0) -> dict:
    key_of = jax.random.split(jax.random.key(seed), 6)
    part_splits = jax.random.split(jax.random.fold_in(key_of[5], part), 6)
    queries = draw_queries(jax.random.fold_in(jax.random.fold_in(key_of[5], part), 71), part)
    keys = draw_keys(jax.random.fold_in(jax.random.fold_in(key_of[5], part), 71), part)
    values = noise(part_splits[2], (TOKENS, FEATURES), 1.0, 6.0, ((0, 64),))
    out_grad = noise(part_splits[3], (TOKENS, FEATURES), 1.0, 6.0, ((0, 64),))
    offsets = draw_offsets(jax.random.fold_in(jax.random.fold_in(key_of[5], part), 71), part)
    return {"queries": queries, "keys": keys, "values": values, "out_grad": out_grad, "offsets": offsets}


very_low = -1e+30

def pick_rows(block, row_offsets, dilation):
    heads = block.shape[1]
    shaped = block.reshape((block.shape[0] // dilation, dilation) + block.shape[1:])
    chosen = lax.broadcasted_iota(jnp.int32, (dilation, heads), 0) == row_offsets[None, :]
    chosen = chosen.reshape((1, dilation, heads) + (1,) * (block.ndim - 2))
    return lax.optimization_barrier(jnp.sum(jnp.where(chosen, shaped, jnp.zeros((), block.dtype)), axis=1))

def spread_rows(values, row_offsets, dilation):
    heads = values.shape[1]
    chosen = lax.broadcasted_iota(jnp.int32, (dilation, heads), 0) == row_offsets[None, :]
    chosen = chosen.reshape((1, dilation, heads) + (1,) * (values.ndim - 2))
    widened = jnp.where(chosen, values[:, None], jnp.zeros((), values.dtype))
    return widened.reshape((values.shape[0] * dilation,) + values.shape[1:])

def chosen_rows(count, row_offsets, dilation):
    places = lax.broadcasted_iota(jnp.int32, (count, row_offsets.shape[0]), 0)
    return places % dilation == row_offsets[None, :]

def merge_levels(level_outs, level_totals, level_masks):
    peak = level_totals[0]
    for total, mask in zip(level_totals[1:], level_masks[1:]):
        peak = jnp.maximum(peak, jnp.where(mask, total, very_low))
    shares = [jnp.exp(jnp.where(mask, total - peak, very_low)) for total, mask in zip(level_totals, level_masks)]
    denominator = shares[0]
    for share in shares[1:]:
        denominator = denominator + share
    merged = level_outs[0] * (shares[0] / denominator)[..., None]
    for mixed, share in zip(level_outs[1:], shares[1:]):
        merged = merged + mixed * (share / denominator)[..., None]
    return (merged, peak + jnp.log(denominator))

def attend(query_blocks, key_blocks, value_blocks, scale):
    scores = jnp.einsum('bmhd,bnhd->bhmn', query_blocks.astype(jnp.float32), key_blocks.astype(jnp.float32)) * scale
    peak = lax.optimization_barrier(jnp.max(scores, axis=3, keepdims=True))
    level_total = peak + jnp.log(lax.optimization_barrier(jnp.sum(jnp.exp(scores - peak), axis=3, keepdims=True)))
    weights = jnp.exp(scores - level_total).astype(jnp.bfloat16)
    weights = lax.optimization_barrier(weights).astype(jnp.float32)
    mixed = jnp.einsum('bhmn,bnhd->bmhd', weights, value_blocks.astype(jnp.float32))
    return (mixed, jnp.transpose(level_total[..., 0], (0, 2, 1)))

def all_grads(query_blocks, key_blocks, value_blocks, grad_blocks, stat_blocks, scale):
    query_wide = query_blocks.astype(jnp.float32)
    key_wide = key_blocks.astype(jnp.float32)
    value_wide = value_blocks.astype(jnp.float32)
    grad_wide = grad_blocks.astype(jnp.float32)
    scores = jnp.einsum('bmhd,bnhd->bhmn', query_wide, key_wide) * scale
    log_total = jnp.transpose(stat_blocks[..., 0], (0, 2, 1))[..., None]
    delta = jnp.transpose(stat_blocks[..., 1], (0, 2, 1))[..., None]
    chance = jnp.exp(scores - log_total)
    prob_grad = jnp.einsum('bmhd,bnhd->bhmn', grad_wide, value_wide)
    score_grad = (chance * (prob_grad - delta) * scale).astype(jnp.bfloat16)
    score_grad = lax.optimization_barrier(score_grad).astype(jnp.float32)
    chance_rounded = lax.optimization_barrier(chance.astype(jnp.bfloat16)).astype(jnp.float32)
    query_grad = jnp.einsum('bhmn,bnhd->bmhd', score_grad, key_wide)
    key_grad = jnp.einsum('bhmn,bmhd->bnhd', score_grad, query_wide)
    value_grad = jnp.einsum('bhmn,bmhd->bnhd', chance_rounded, grad_wide)
    return (query_grad, key_grad, value_grad)

def reference(queries, keys, values, out_grad, offsets):
    tokens, features = queries.shape
    levels, heads = offsets.shape
    width = features // heads
    scale = 1.0 / math.sqrt(width)
    seg_rows = tokens // 2 ** (levels - 1)
    query4 = queries.reshape(tokens, heads, width)
    key4 = keys.reshape(tokens, heads, width)
    value4 = values.reshape(tokens, heads, width)
    grad4 = out_grad.reshape(tokens, heads, width)
    picked_all = []
    level_outs, level_totals, level_masks = ([], [], [])
    for level in range(levels):
        dilation = 2 ** level
        row_offsets = offsets[level]
        picked = tuple((pick_rows(block, row_offsets, dilation) for block in (query4, key4, value4, grad4)))
        picked_all.append(picked)
        count = tokens // dilation // seg_rows
        rows = tokens // dilation
        blocks = tuple((block.reshape(count, 1, seg_rows, heads, width) for block in picked[:3]))
        mixed, level_total = lax.map(lambda parts: attend(parts[0], parts[1], parts[2], scale), blocks)
        level_outs.append(spread_rows(mixed.reshape(rows, heads, width), row_offsets, dilation))
        level_totals.append(spread_rows(level_total.reshape(rows, heads), row_offsets, dilation))
        level_masks.append(chosen_rows(tokens, row_offsets, dilation))
    merged, log_total = merge_levels(level_outs, level_totals, level_masks)
    attended = merged.astype(jnp.bfloat16).reshape(tokens, features)
    delta = lax.optimization_barrier(jnp.sum(grad4.astype(jnp.float32) * merged, axis=2))
    stats = jnp.stack([log_total, delta], axis=2)
    query_sum = jnp.zeros((tokens, heads, width), jnp.float32)
    key_sum = jnp.zeros((tokens, heads, width), jnp.float32)
    value_sum = jnp.zeros((tokens, heads, width), jnp.float32)
    for level in range(levels):
        dilation = 2 ** level
        row_offsets = offsets[level]
        count = tokens // dilation // seg_rows
        rows = tokens // dilation
        picked = picked_all[level] + (pick_rows(stats, row_offsets, dilation),)
        blocks = tuple((block.reshape((count, 1, seg_rows) + block.shape[1:]) for block in picked))
        grads = lax.map(lambda parts: all_grads(parts[0], parts[1], parts[2], parts[3], parts[4], scale), blocks)
        query_sum = query_sum + spread_rows(grads[0].reshape(rows, heads, width), row_offsets, dilation)
        key_sum = key_sum + spread_rows(grads[1].reshape(rows, heads, width), row_offsets, dilation)
        value_sum = value_sum + spread_rows(grads[2].reshape(rows, heads, width), row_offsets, dilation)
    return (attended, query_sum.astype(jnp.bfloat16).reshape(tokens, features), key_sum.astype(jnp.bfloat16).reshape(tokens, features), value_sum.astype(jnp.bfloat16).reshape(tokens, features))
```

```python
import math

import jax
import jax.numpy as jnp
from jax import lax
from jax.experimental import pallas as pl
from jax.experimental.pallas import tpu as pltpu
from jax.sharding import PartitionSpec as P

HEADS = 8
WIDTH = 128
ROWS = 128
PLANE = HEADS * ROWS
DEPTH = 8
SEG = 256
SCALE = 1.0 / math.sqrt(WIDTH)
F32 = jnp.float32
BF16 = jnp.bfloat16


def nt(a, b):
    return lax.dot_general(a, b, (((1,), (1,)), ((), ())), preferred_element_type=F32)


def nn(a, b):
    return lax.dot_general(a, b, (((1,), (0,)), ((), ())), preferred_element_type=F32)


def tn(a, b):
    return lax.dot_general(a, b, (((0,), (0,)), ((), ())), preferred_element_type=F32)


def attend(q, k, v):
    scores = nt(q, k) * SCALE
    peak = jnp.max(scores, axis=1, keepdims=True)
    grown = jnp.exp(scores - peak)
    mass = jnp.sum(grown, axis=1, keepdims=True)
    weights = (grown * (1.0 / mass)).astype(BF16)
    return nn(weights, v), peak + jnp.log(mass)


def merge(out, total, more, more_total):
    peak = jnp.maximum(total, more_total)
    joined = peak + jnp.log(jnp.exp(total - peak) + jnp.exp(more_total - peak))
    return out * jnp.exp(total - joined) + more * jnp.exp(more_total - joined), joined


def wide(column, rows):
    return jnp.broadcast_to(column, (rows, WIDTH))


def chosen(offs):
    return (
        pl.ds(offs[5], 32, stride=32),
        pl.ds(offs[5] ^ 16, 32, stride=32),
        pl.ds(offs[4] ^ 8, 64, stride=16),
    )


def load_chosen(ref, offs):
    return jnp.concatenate([ref[s, :] for s in chosen(offs)], axis=0)


def store_chosen(ref, offs, rows):
    first, second, third = chosen(offs)
    ref[first, :] = rows[:32]
    ref[second, :] = rows[32:64]
    ref[third, :] = rows[64:]


def pick_kernel(offs, x, g, wide_rows):
    for t in range(4):
        wide_rows[...] = x[:, t].reshape(PLANE, WIDTH).astype(F32)
        g[t] = load_chosen(wide_rows, offs).astype(BF16)


def near_kernel(offs, x, o, t, qs, ks, vs):
    for index, ref in enumerate((qs, ks, vs)):
        ref[...] = x[:, index].reshape(PLANE, WIDTH).astype(F32)
    for s in range(4):
        q, k, v = (x[2 * s : 2 * s + 2, index].reshape(SEG, WIDTH) for index in range(3))
        out, total = attend(q, k, v)
        o[s * SEG : (s + 1) * SEG] = out
        t[s * SEG : (s + 1) * SEG] = wide(total, SEG)
    for level, begin in ((1, 0), (1, 512), (2, 0)):
        rows = pl.ds(offs[level] + begin, SEG, stride=2**level)
        q, k, v = (ref[rows, :].astype(BF16) for ref in (qs, ks, vs))
        out, total = attend(q, k, v)
        out, total = merge(o[rows, :], t[rows, :], out, wide(total, SEG))
        o[rows, :] = out
        t[rows, :] = total


def far_blocks(g, a1, a2, a3, index):
    own = g[index]
    three = jnp.concatenate([own, a1[index]], axis=0)
    four = jnp.concatenate([own[:64], a1[index, :64], a2[0, index], a2[1, index]], axis=0)
    five = jnp.concatenate(
        [own[:32], a1[index, :32], a2[0, index, :32], a2[1, index, :32]]
        + [a3[z, index] for z in range(4)],
        axis=0,
    )
    return three, four, five


def far_kernel(offs, x, g, a1, a2, a3, o_in, t_in, att, stats, message, o, t):
    keys, values = (far_blocks(g, a1, a2, a3, index) for index in (1, 2))
    out, total = load_chosen(o_in, offs), load_chosen(t_in, offs)
    for level in range(3):
        rows = 128 >> level
        more, more_total = attend(g[0][:rows], keys[level], values[level])
        part, part_total = merge(out[:rows], total[:rows], more, wide(more_total, rows))
        if level:
            part = jnp.concatenate([part, out[rows:]], axis=0)
            part_total = jnp.concatenate([part_total, total[rows:]], axis=0)
        out, total = part, part_total
    o[...] = o_in[...]
    t[...] = t_in[...]
    store_chosen(o, offs, out)
    store_chosen(t, offs, total)
    merged = o[...]
    att[...] = merged.astype(BF16).reshape(HEADS, ROWS, WIDTH)
    delta = jnp.sum(merged * x[:, 3].reshape(PLANE, WIDTH).astype(F32), axis=1, keepdims=True)
    lane = lax.broadcasted_iota(jnp.int32, (PLANE, WIDTH), 1)
    stats[...] = jnp.where(lane % 8 < 4, t[...], delta)
    message[...] = load_chosen(stats, offs).T[:8]


def score_parts(q, k, v, do, stat):
    chance = jnp.exp(nt(q, k) * SCALE - stat[:, 0:1])
    score = (chance * (nt(do, v) - stat[:, 4:5]) * SCALE).astype(BF16)
    return chance.astype(BF16), score


def back_kernel(offs, x, g, a1, a2, a3, stats, dq_out, dk, dv, qs, ks, vs, ds, dq):
    for index, ref in enumerate((qs, ks, vs, ds)):
        ref[...] = x[:, index].reshape(PLANE, WIDTH).astype(F32)
    for s in range(4):
        rows = slice(s * SEG, (s + 1) * SEG)
        q, k, v, do = (x[2 * s : 2 * s + 2, index].reshape(SEG, WIDTH) for index in range(4))
        chance, score = score_parts(q, k, v, do, stats[rows])
        dq[rows] = nn(score, k)
        dk[rows] = tn(score, q)
        dv[rows] = tn(chance, do)
    for level, begin in ((1, 0), (1, 512), (2, 0)):
        rows = pl.ds(offs[level] + begin, SEG, stride=2**level)
        q, k, v, do = (ref[rows, :].astype(BF16) for ref in (qs, ks, vs, ds))
        chance, score = score_parts(q, k, v, do, stats[rows, :])
        dq[rows, :] = dq[rows, :] + nn(score, k)
        dk[rows, :] = dk[rows, :] + tn(score, q)
        dv[rows, :] = dv[rows, :] + tn(chance, do)
    keys, values = (far_blocks(g, a1, a2, a3, index) for index in (1, 2))
    stat = load_chosen(stats, offs)
    total = load_chosen(dq, offs)
    for level in range(3):
        rows = 128 >> level
        _, score = score_parts(g[0][:rows], keys[level], values[level], g[3][:rows], stat[:rows])
        part = total[:rows] + nn(score, keys[level])
        total = jnp.concatenate([part, total[rows:]], axis=0) if level else part
    store_chosen(dq, offs, total)
    dq_out[...] = dq[...].astype(BF16).reshape(HEADS, ROWS, WIDTH)


def far_stats(m0, m1, m2, m3):
    lane = lax.broadcasted_iota(jnp.int32, (8, WIDTH), 1)

    def pair(a, b):
        return jnp.where(lane < 64, a, pltpu.roll(b, 64, 1))

    def four(a, b, c, d):
        return jnp.where(
            lane < 64,
            jnp.where(lane < 32, a, pltpu.roll(b, 32, 1)),
            jnp.where(lane < 96, pltpu.roll(c, 64, 1), pltpu.roll(d, 96, 1)),
        )

    three = jnp.concatenate([m0, m1], axis=1)
    wider = jnp.concatenate([pair(m0, m1), pair(m2[0], m2[1])], axis=1)
    widest = jnp.concatenate([four(m0, m1, m2[0], m2[1]), four(m3[0], m3[1], m3[2], m3[3])], axis=1)
    return three, wider, widest


def keys_kernel(offs, g, a1, a2, a3, m0, m1, m2, m3, dk_in, dv_in, dk_out, dv_out, dk, dv):
    queries, grads = (far_blocks(g, a1, a2, a3, index) for index in (0, 3))
    stats = far_stats(m0[...], m1[...], m2[...], m3[...])
    dk[...] = dk_in[...]
    dv[...] = dv_in[...]
    key_total, value_total = load_chosen(dk, offs), load_chosen(dv, offs)
    for level in range(3):
        rows = 128 >> level
        chance = jnp.exp(nt(g[1][:rows], queries[level]) * SCALE - stats[level][0:1])
        score = (chance * (nt(g[2][:rows], grads[level]) - stats[level][4:5]) * SCALE).astype(BF16)
        key_part = key_total[:rows] + nn(score, queries[level])
        value_part = value_total[:rows] + nn(chance.astype(BF16), grads[level])
        if level:
            key_part = jnp.concatenate([key_part, key_total[rows:]], axis=0)
            value_part = jnp.concatenate([value_part, value_total[rows:]], axis=0)
        key_total, value_total = key_part, value_part
    store_chosen(dk, offs, key_total)
    store_chosen(dv, offs, value_total)
    dk_out[...] = dk[...].astype(BF16).reshape(HEADS, ROWS, WIDTH)
    dv_out[...] = dv[...].astype(BF16).reshape(HEADS, ROWS, WIDTH)


def call(kernel, name, outs, scratch, *args):
    smem = pl.BlockSpec(memory_space=pltpu.SMEM)
    vmem = pl.BlockSpec(memory_space=pltpu.VMEM)
    return pl.pallas_call(
        kernel,
        name=name,
        out_shape=tuple(jax.ShapeDtypeStruct(shape, dtype) for shape, dtype in outs),
        in_specs=[smem] + [vmem] * (len(args) - 1),
        out_specs=(vmem,) * len(outs),
        scratch_shapes=[pltpu.VMEM(shape, F32) for shape in scratch],
        compiler_params=pltpu.CompilerParams(vmem_limit_bytes=40 * 2**20),
    )(*args)


def across(array, flip):
    moves = [(HEADS * z + i, HEADS * (z ^ flip) + i) for z in range(DEPTH) for i in range(HEADS)]
    return lax.ppermute(array, "ctx", moves)


def planes():
    return [[HEADS * z + i for i in range(HEADS)] for z in range(DEPTH)]


def shards(queries, keys, values, out_grad, offsets):
    head = lax.axis_index("ctx") % HEADS
    offs = lax.dynamic_index_in_dim(offsets, head, axis=1, keepdims=False)
    stacked = jnp.stack(
        [a.reshape(ROWS, HEADS, WIDTH).transpose(1, 0, 2) for a in (queries, keys, values, out_grad)],
        axis=1,
    )
    x = lax.all_to_all(stacked, "ctx", 0, 0, axis_index_groups=planes(), tiled=True)
    full = (PLANE, WIDTH)
    blocks = (HEADS, ROWS, WIDTH)
    (g,) = call(pick_kernel, "pick", [((4, ROWS, WIDTH), BF16)], [full], offs, x)
    a1 = across(g, 1)
    a2 = across(jnp.stack([g[:, :64], a1[:, :64]]), 3)
    a3 = across(jnp.concatenate([jnp.stack([g[:, :32], a1[:, :32]]), a2[:, :, :32]]), 7)
    o, t = call(near_kernel, "near", [(full, F32), (full, F32)], [full] * 3, offs, x)
    att, stats, m0 = call(
        far_kernel,
        "far",
        [(blocks, BF16), (full, F32), ((8, WIDTH), F32)],
        [full] * 2,
        offs, x, g, a1, a2, a3, o, t,
    )
    m1 = across(m0, 1)
    m2 = across(jnp.stack([m0, m1]), 3)
    m3 = across(jnp.concatenate([jnp.stack([m0, m1]), m2]), 7)
    dq, dk, dv = call(
        back_kernel,
        "back",
        [(blocks, BF16), (full, F32), (full, F32)],
        [full] * 5,
        offs, x, g, a1, a2, a3, stats,
    )
    dk, dv = call(
        keys_kernel,
        "keys",
        [(blocks, BF16), (blocks, BF16)],
        [full] * 2,
        offs, g, a1, a2, a3, m0, m1, m2, m3, dk, dv,
    )
    back = lax.all_to_all(
        jnp.stack([att, dq, dk, dv], axis=1), "ctx", 0, 0, axis_index_groups=planes(), tiled=True
    )
    return tuple(back[:, i].transpose(1, 0, 2).reshape(ROWS, HEADS * WIDTH) for i in range(4))


def solution(mesh):
    rows = P(("dp", "ctx"), None)
    return jax.shard_map(
        shards,
        mesh=mesh,
        in_specs=(rows,) * 4 + (P("dp", None),),
        out_specs=(rows,) * 4,
        check_vma=False,
    )
```

```python
import math

import jax
import jax.numpy as jnp
from jax import lax
from jax.experimental import pallas as pl
from jax.experimental.pallas import tpu as pltpu
from jax.sharding import PartitionSpec as P

HEADS = 8
WIDTH = 128
ROWS = 128
CHIP = 2 * ROWS
CHIPS = 4
PLANE = 2 * CHIPS
DEPTH = 8
SEG = 256
BODY = 4 * ROWS
MESSAGE = BODY + 32
SCALE = 1.0 / math.sqrt(WIDTH)
F32 = jnp.float32
BF16 = jnp.bfloat16


def nt(a, b):
    return lax.dot_general(a, b, (((1,), (1,)), ((), ())), preferred_element_type=F32)


def nn(a, b):
    return lax.dot_general(a, b, (((1,), (0,)), ((), ())), preferred_element_type=F32)


def tn(a, b):
    return lax.dot_general(a, b, (((0,), (0,)), ((), ())), preferred_element_type=F32)


def join(parts):
    return jnp.concatenate(parts, axis=0)


def attend(q, k, v):
    scores = nt(q, k) * SCALE
    peak = jnp.max(scores, axis=1, keepdims=True)
    grown = jnp.exp(scores - peak)
    mass = jnp.sum(grown, axis=1, keepdims=True)
    weights = (grown * (1.0 / mass)).astype(BF16)
    return nn(weights, v), peak + jnp.log(mass)


def dotted(a, b):
    return jnp.sum(a.astype(F32) * b, axis=1, keepdims=True)


def mixed(total, delta):
    rows = total.shape[0]
    lane = lax.broadcasted_iota(jnp.int32, (rows, WIDTH), 1)
    return jnp.where(lane % 8 < 4, total, delta)


def total_of(stat):
    return stat[:, 0:1]


def delta_of(stat):
    return stat[:, 4:5]


def combine(stat, total, delta):
    old = total_of(stat)
    peak = jnp.maximum(old, total)
    joined = peak + jnp.log(jnp.exp(old - peak) + jnp.exp(total - peak))
    kept, added = jnp.exp(old - joined), jnp.exp(total - joined)
    return mixed(joined, kept * delta_of(stat) + added * delta), kept, added


def pack(stat):
    flat = stat.T[:8]
    high = flat.astype(BF16).astype(F32)
    middle = (flat - high).astype(BF16).astype(F32)
    low = flat - high - middle
    return join([high, middle, low, jnp.zeros_like(low)]).astype(BF16)


def unpack(rows):
    terms = rows.astype(F32)
    flat = terms[:8] + terms[8:16] + terms[16:24]
    return join([flat] * 16).T


def score_parts(q, k, v, do, stat):
    chance = jnp.exp(nt(q, k) * SCALE - total_of(stat))
    score = (chance * (nt(do, v) - delta_of(stat)) * SCALE).astype(BF16)
    return chance.astype(BF16), score


def chosen(offs, head):
    return (
        (0, pl.ds(offs[5, head], 8, stride=32)),
        (8, pl.ds(offs[5, head] ^ 16, 8, stride=32)),
        (16, pl.ds(offs[4, head] ^ 8, 16, stride=16)),
        (32, pl.ds(offs[3, head] ^ 4, 32, stride=8)),
        (64, pl.ds(offs[2, head] ^ 2, 64, stride=4)),
    )


def load_chosen(ref, offs, head):
    return join([ref[rows, :] for _, rows in chosen(offs, head)])


def lanes(head):
    return pl.ds(pl.multiple_of(head * WIDTH, WIDTH), WIDTH)


def split_kernel(place, q, k, v, do, theirs):
    for y in range(CHIPS):
        for t, ref in enumerate((q, k, v, do)):
            theirs[y, t] = ref[:, lanes(2 * y + 1 - place[0])]


def chip_rows(place, step, raw, theirs):
    y = place[1] ^ step
    head = 2 * y + place[0]
    return head, [join([ref[:, lanes(head)], theirs[y, t]]) for t, ref in enumerate(raw)]


def chip_kernel(offs, place, q, k, v, do, theirs, m0, m1, m2, m3, outs, stats, work):
    for step, message in enumerate((m0, m1, m2, m3)):
        head, tensors = chip_rows(place, step, (q, k, v, do), theirs)
        out, total = attend(*tensors[:3])
        stat = mixed(total, dotted(tensors[3], out))
        outs[step] = out
        stats[step] = stat
        for t, rows in enumerate(tensors):
            work[t] = rows.astype(F32)
            message[t * ROWS : (t + 1) * ROWS] = load_chosen(work.at[t], offs, head).astype(BF16)
        work[4] = stat
        message[BODY:] = pack(load_chosen(work.at[4], offs, head))


def tensor(ref, t, rows=ROWS):
    return ref[t * ROWS : t * ROWS + rows]


def group(parts):
    return join(
        [p[:8] for p in parts] + [p[8:16] for p in parts] + [p[16:32] for p in parts]
    )


def ungroup(rows, chip):
    return join(
        [
            rows[8 * chip : 8 * chip + 8],
            rows[32 + 8 * chip : 40 + 8 * chip],
            rows[64 + 16 * chip : 80 + 16 * chip],
        ]
    )


def near_kernel(m0, m1, m2, m3, outs, stats, g):
    refs = (m0, m1, m2, m3)
    stat = [unpack(ref[BODY:]) for ref in refs]
    out = [None] * 4
    for pair in (0, 2):
        q, k, v, do = (join([tensor(refs[pair], t), tensor(refs[pair + 1], t)]) for t in range(4))
        more, total = attend(q, k, v)
        joined, _, added = combine(join(stat[pair : pair + 2]), total, dotted(do, more))
        more = more * added
        for chip in range(2):
            out[pair + chip] = more[chip * ROWS : (chip + 1) * ROWS]
            stat[pair + chip] = joined[chip * ROWS : (chip + 1) * ROWS]
    q, k, v, do = (join([tensor(ref, t, 64) for ref in refs]) for t in range(4))
    more, total = attend(q, k, v)
    joined, kept, added = combine(join([s[:64] for s in stat]), total, dotted(do, more))
    more = join([o[:64] for o in out]) * kept + more * added
    for chip in range(4):
        out[chip] = join([more[chip * 64 : (chip + 1) * 64], out[chip][64:]])
        stat[chip] = join([joined[chip * 64 : (chip + 1) * 64], stat[chip][64:]])
        outs[chip] = out[chip]
        stats[chip] = stat[chip]
    for t in range(4):
        rows = group([tensor(ref, t, 32).astype(F32) for ref in refs])
        g[t * ROWS : (t + 1) * ROWS] = rows.astype(BF16)
    g[BODY:] = pack(group(stat))


def far_kernel(g, a1, a2, a3, out_far, stats, message):
    refs = (g, a1, a2, a3)
    stat = [unpack(ref[BODY:]) for ref in refs]
    out = None
    for pair in (0, 2):
        q, k, v, do = (join([tensor(refs[pair], t), tensor(refs[pair + 1], t)]) for t in range(4))
        more, total = attend(q, k, v)
        joined, _, added = combine(join(stat[pair : pair + 2]), total, dotted(do, more))
        stat[pair], stat[pair + 1] = joined[:ROWS], joined[ROWS:]
        if pair == 0:
            out = (more * added)[:ROWS]
    q, k, v, do = (join([tensor(ref, t, 64) for ref in refs]) for t in range(4))
    more, total = attend(q, k, v)
    joined, kept, added = combine(join([s[:64] for s in stat]), total, dotted(do, more))
    out_far[...] = join([out[:64] * kept[:64] + more[:64] * added[:64], out[64:]])
    for z in range(4):
        stat[z] = join([joined[z * 64 : (z + 1) * 64], stat[z][64:]])
        stats[z] = stat[z]
    message[...] = join([s[:32] for s in stat]).T[:8]


def rest_kernel(
    m0, m1, m2, m3, outs, stats, g, a1, a2, a3, out_far, stats_far, far5, message5, c0, c1, c2, c3
):
    refs, fars = (m0, m1, m2, m3), (g, a1, a2, a3)
    own = [tensor(g, t) for t in range(4)]
    three = [join([tensor(g, t), tensor(a1, t)]) for t in range(4)]
    four = [join([tensor(ref, t, 64) for ref in fars]) for t in range(4)]
    five = [
        join([tensor(ref, t, 32) for ref in fars] + [far5[z, t] for z in range(4)])
        for t in range(4)
    ]
    far = [stats_far[z] for z in range(4)]
    more, total = attend(*five[:3])
    old = join([s[:32] for s in far] + [join([message5[...]] * 16).T])
    stat5, kept, added = combine(old, total, dotted(five[3], more))
    stat4 = join([join([stat5[32 * z : 32 * z + 32], far[z][32:64]]) for z in range(4)])
    stat3 = join([join([stat5[32 * z : 32 * z + 32], far[z][32:]]) for z in range(2)])
    own_stat = stat3[:ROWS]
    out = join([out_far[:32] * kept[:32] + more[:32] * added[:32], out_far[32:]])
    near = group([stats[chip] for chip in range(4)])
    out = out + group([outs[chip] for chip in range(4)]) * jnp.exp(
        total_of(near) - total_of(own_stat)
    )
    dq = dk = dv = None
    for level, (rows, gathered, stat) in enumerate(
        ((128, three, stat3), (64, four, stat4), (32, five, stat5))
    ):
        _, score = score_parts(
            own[0][:rows], gathered[1], gathered[2], own[3][:rows], own_stat[:rows]
        )
        queries = nn(score, gathered[1])
        chance, score = score_parts(
            gathered[0], own[1][:rows], own[2][:rows], gathered[3], stat
        )
        keys, values = tn(score, gathered[0]), tn(chance, gathered[3])
        if level == 0:
            dq, dk, dv = queries, keys, values
        else:
            dq, dk, dv = (
                join([whole[:rows] + part, whole[rows:]])
                for whole, part in ((dq, queries), (dk, keys), (dv, values))
            )
    stat = [join([ungroup(own_stat, chip), stats[chip, 32:]]) for chip in range(4)]
    sums = [None] * 4
    for pair in (0, 2):
        q, k, v, do = (join([tensor(refs[pair], t), tensor(refs[pair + 1], t)]) for t in range(4))
        chance, score = score_parts(q, k, v, do, join(stat[pair : pair + 2]))
        parts = nn(score, k), tn(score, q), tn(chance, do)
        for chip in range(2):
            sums[pair + chip] = [part[chip * ROWS : (chip + 1) * ROWS] for part in parts]
    q, k, v, do = (join([tensor(ref, t, 64) for ref in refs]) for t in range(4))
    chance, score = score_parts(q, k, v, do, join([s[:64] for s in stat]))
    parts = nn(score, k), tn(score, q), tn(chance, do)
    for chip, message in enumerate((c0, c1, c2, c3)):
        message[:ROWS] = join([ungroup(out, chip), outs[chip, 32:]]).astype(BF16)
        for t, (whole, part, top) in enumerate(zip(sums[chip], parts, (dq, dk, dv))):
            part = part[chip * 64 : (chip + 1) * 64]
            rows = join(
                [whole[:32] + part[:32] + ungroup(top, chip), whole[32:64] + part[32:], whole[64:]]
            )
            message[(t + 1) * ROWS : (t + 2) * ROWS] = rows.astype(BF16)
        message[BODY:] = pack(stat[chip])


def finish_kernel(
    offs, place, q, k, v, do, theirs, outs, stats, c0, c1, c2, c3, mine_out, theirs_out, work
):
    for step, message in enumerate((c0, c1, c2, c3)):
        head, tensors = chip_rows(place, step, (q, k, v, do), theirs)
        places = chosen(offs, head)
        work[4] = stats[step]
        final = unpack(message[BODY:])
        for begin, rows in places:
            work[4, rows, :] = final[begin : begin + rows.size]
        stat = work[4]
        work[0] = outs[step] * jnp.exp(total_of(stats[step]) - total_of(stat))
        chance, score = score_parts(*tensors, stat)
        work[1] = nn(score, tensors[1])
        work[2] = tn(score, tensors[0])
        work[3] = tn(chance, tensors[3])
        for t in range(4):
            part = tensor(message, t).astype(F32)
            for begin, rows in places:
                work[t, rows, :] = work[t, rows, :] + part[begin : begin + rows.size]
            mine_out[step, t] = work[t, :ROWS].astype(BF16)
            theirs_out[step, t] = work[t, ROWS:].astype(BF16)


def place_kernel(place, mine, theirs, att, dq, dk, dv):
    for step in range(CHIPS):
        head = 2 * (place[1] ^ step)
        for t, ref in enumerate((att, dq, dk, dv)):
            ref[:, lanes(head + place[0])] = mine[step, t]
            ref[:, lanes(head + 1 - place[0])] = theirs[step, t]


def call(kernel, name, scalars, outs, scratch, *args):
    smem = pl.BlockSpec(memory_space=pltpu.SMEM)
    vmem = pl.BlockSpec(memory_space=pltpu.VMEM)
    return pl.pallas_call(
        kernel,
        name=name,
        out_shape=tuple(jax.ShapeDtypeStruct(shape, dtype) for shape, dtype in outs),
        in_specs=[smem] * scalars + [vmem] * (len(args) - scalars),
        out_specs=(vmem,) * len(outs),
        scratch_shapes=[pltpu.VMEM(shape, F32) for shape in scratch],
        compiler_params=pltpu.CompilerParams(vmem_limit_bytes=40 * 2**20),
    )(*args)


def in_plane(array, flip):
    moves = [(PLANE * z + i, PLANE * z + (i ^ flip)) for z in range(DEPTH) for i in range(PLANE)]
    return lax.ppermute(array, "ctx", moves)


def across(array, flip):
    moves = [(PLANE * z + i, PLANE * (z ^ flip) + i) for z in range(DEPTH) for i in range(PLANE)]
    return lax.ppermute(array, "ctx", moves)


def shards(queries, keys, values, out_grad, offsets):
    spot = lax.axis_index("ctx") % PLANE
    place = jnp.stack([spot % 2, spot // 2])
    raw = (queries, keys, values, out_grad)
    half = ((CHIPS, 4, ROWS, WIDTH), BF16)
    message = ((MESSAGE, WIDTH), BF16)
    quads = ((4, ROWS, WIDTH), F32)
    chips = ((4, CHIP, WIDTH), F32)
    (theirs,) = call(split_kernel, "split", 1, [half], [], place, *raw)
    theirs = in_plane(theirs, 1)
    *sent, outs0, stats0 = call(
        chip_kernel, "chip", 2, [message] * 4 + [chips] * 2, [(5, CHIP, WIDTH)],
        offsets, place, *raw, theirs,
    )
    got = [sent[0]] + [in_plane(sent[step], 2 * step) for step in (1, 2, 3)]
    outs, stats, g = call(near_kernel, "near", 0, [quads, quads, message], [], *got)
    fars = [g] + [across(g, flip) for flip in (1, 2, 3)]
    top = jnp.stack([far[:BODY].reshape(4, ROWS, WIDTH)[:, :32] for far in fars])
    top = across(top, 7)
    out_far, stats_far, message5 = call(
        far_kernel, "far", 0, [((ROWS, WIDTH), F32), quads, ((8, WIDTH), F32)], [], *fars
    )
    message5 = across(message5, 7)
    back = call(
        rest_kernel, "rest", 0, [message] * 4, [],
        *got, outs, stats, *fars, out_far, stats_far, top, message5,
    )
    back = [back[0]] + [in_plane(back[step], 2 * step) for step in (1, 2, 3)]
    mine, theirs_out = call(
        finish_kernel, "finish", 2, [half, half], [(5, CHIP, WIDTH)],
        offsets, place, *raw, theirs, outs0, stats0, *back,
    )
    theirs_out = in_plane(theirs_out, 1)
    row = ((ROWS, HEADS * WIDTH), BF16)
    return call(place_kernel, "place", 1, [row] * 4, [], place, mine, theirs_out)


def solution(mesh):
    rows = P(("dp", "ctx"), None)
    return jax.shard_map(
        shards,
        mesh=mesh,
        in_specs=(rows,) * 4 + (P("dp", None),),
        out_specs=(rows,) * 4,
        check_vma=False,
    )
```

```python
import functools
import math

import jax
import jax.numpy as jnp
from jax import lax
from jax.experimental import pallas as pl
from jax.experimental.pallas import tpu as pltpu
from jax.sharding import PartitionSpec as P

HEADS = 8
WIDTH = 128
ROWS = 128
CHIP = 2 * ROWS
CHIPS = 4
PLANE = 2 * CHIPS
DEPTH = 8
SEG = 256
BODY = 4 * ROWS
MESSAGE = BODY + 32
SCALE = 1.0 / math.sqrt(WIDTH)
F32 = jnp.float32
BF16 = jnp.bfloat16


def nt(a, b):
    return lax.dot_general(a, b, (((1,), (1,)), ((), ())), preferred_element_type=F32)


def nn(a, b):
    return lax.dot_general(a, b, (((1,), (0,)), ((), ())), preferred_element_type=F32)


def tn(a, b):
    return lax.dot_general(a, b, (((0,), (0,)), ((), ())), preferred_element_type=F32)


def join(parts):
    return jnp.concatenate(parts, axis=0)


def attend(q, k, v):
    scores = nt(q, k) * SCALE
    peak = jnp.max(scores, axis=1, keepdims=True)
    grown = jnp.exp(scores - peak)
    mass = jnp.sum(grown, axis=1, keepdims=True)
    weights = (grown * (1.0 / mass)).astype(BF16)
    return nn(weights, v), peak + jnp.log(mass)


def dotted(a, b):
    return jnp.sum(a.astype(F32) * b, axis=1, keepdims=True)


def mixed(total, delta):
    rows = total.shape[0]
    lane = lax.broadcasted_iota(jnp.int32, (rows, WIDTH), 1)
    return jnp.where(lane % 8 < 4, total, delta)


def total_of(stat):
    return stat[:, 0:1]


def delta_of(stat):
    return stat[:, 4:5]


def combine(stat, total, delta):
    old = total_of(stat)
    peak = jnp.maximum(old, total)
    joined = peak + jnp.log(jnp.exp(old - peak) + jnp.exp(total - peak))
    kept, added = jnp.exp(old - joined), jnp.exp(total - joined)
    return mixed(joined, kept * delta_of(stat) + added * delta), kept, added


def pack(stat):
    flat = stat.T[:8]
    high = flat.astype(BF16).astype(F32)
    middle = (flat - high).astype(BF16).astype(F32)
    low = flat - high - middle
    return join([high, middle, low, jnp.zeros_like(low)]).astype(BF16)


def unpack(rows):
    terms = rows.astype(F32)
    flat = terms[:8] + terms[8:16] + terms[16:24]
    return join([flat] * 16).T


def score_parts(q, k, v, do, stat):
    chance = jnp.exp(nt(q, k) * SCALE - total_of(stat))
    score = (chance * (nt(do, v) - delta_of(stat)) * SCALE).astype(BF16)
    return chance.astype(BF16), score


def chosen(offs, head):
    return (
        (0, pl.ds(offs[5, head], 8, stride=32)),
        (8, pl.ds(offs[5, head] ^ 16, 8, stride=32)),
        (16, pl.ds(offs[4, head] ^ 8, 16, stride=16)),
        (32, pl.ds(offs[3, head] ^ 4, 32, stride=8)),
        (64, pl.ds(offs[2, head] ^ 2, 64, stride=4)),
    )


def load_chosen(ref, offs, head):
    return join([ref[rows, :] for _, rows in chosen(offs, head)])


def lanes(head):
    return pl.ds(pl.multiple_of(head * WIDTH, WIDTH), WIDTH)


def own_head(step):
    spot = lax.axis_index("ctx") % PLANE
    return spot ^ (2 * step)


def other_head(step):
    return own_head(step) ^ 1


def split_kernel(q, k, v, do, q_in, k_in, v_in, do_in, theirs, sems):
    inside = (q_in, k_in, v_in, do_in)
    copies = [
        pltpu.make_async_copy(ref, to, sems.at[t])
        for t, (ref, to) in enumerate(zip((q, k, v, do), inside))
    ]
    for copy in copies:
        copy.start()
    for t, ref in enumerate(inside):
        copies[t].wait()
        for step in range(CHIPS):
            theirs[step, t] = ref[:, lanes(other_head(step))]


def chip_rows(step, raw, theirs):
    head = own_head(step)
    return [join([ref[:, lanes(head)], theirs[step, t]]) for t, ref in enumerate(raw)]


def chip_kernel(
    offs_left, q, k, v, do, theirs, m0, m1, m2, m3, outs, stats, work, offs, sem
):
    copy = pltpu.make_async_copy(offs_left, offs, sem.at[0])
    copy.start()
    tensors = [chip_rows(step, (q, k, v, do), theirs) for step in range(CHIPS)]
    for step in range(CHIPS):
        out, total = attend(*tensors[step][:3])
        stat = mixed(total, dotted(tensors[step][3], out))
        outs[step] = out
        stats[step] = stat
        for t in range(4):
            work[step, t] = tensors[step][t].astype(F32)
        work[step, 4] = stat
    copy.wait()
    for step, message in enumerate((m0, m1, m2, m3)):
        head = own_head(step)
        for t in range(4):
            picked = load_chosen(work.at[step, t], offs, head)
            message[t * ROWS : (t + 1) * ROWS] = picked.astype(BF16)
        message[BODY:] = pack(load_chosen(work.at[step, 4], offs, head))


def tensor(ref, t, rows=ROWS):
    return ref[t * ROWS : t * ROWS + rows]


def group(parts):
    return join(
        [p[:8] for p in parts] + [p[8:16] for p in parts] + [p[16:32] for p in parts]
    )


def ungroup(rows, chip):
    return join(
        [
            rows[8 * chip : 8 * chip + 8],
            rows[32 + 8 * chip : 40 + 8 * chip],
            rows[64 + 16 * chip : 80 + 16 * chip],
        ]
    )


def near_kernel(m0, m1, m2, m3, outs, stats, g, g4):
    refs = (m0, m1, m2, m3)
    stat = [unpack(ref[BODY:]) for ref in refs]
    out = [None] * 4
    for pair in (0, 2):
        q, k, v, do = (join([tensor(refs[pair], t), tensor(refs[pair + 1], t)]) for t in range(4))
        more, total = attend(q, k, v)
        joined, _, added = combine(join(stat[pair : pair + 2]), total, dotted(do, more))
        more = more * added
        for chip in range(2):
            out[pair + chip] = more[chip * ROWS : (chip + 1) * ROWS]
            stat[pair + chip] = joined[chip * ROWS : (chip + 1) * ROWS]
    q, k, v, do = (join([tensor(ref, t, 64) for ref in refs]) for t in range(4))
    more, total = attend(q, k, v)
    joined, kept, added = combine(join([s[:64] for s in stat]), total, dotted(do, more))
    more = join([o[:64] for o in out]) * kept + more * added
    for chip in range(4):
        out[chip] = join([more[chip * 64 : (chip + 1) * 64], out[chip][64:]])
        stat[chip] = join([joined[chip * 64 : (chip + 1) * 64], stat[chip][64:]])
        outs[chip] = out[chip]
        stats[chip] = stat[chip]
    for t in range(4):
        rows = group([tensor(ref, t, 32).astype(F32) for ref in refs])
        rows = rows.astype(BF16)
        g[t * ROWS : (t + 1) * ROWS] = rows
        g4[t] = rows[:64]
    g[BODY:] = pack(group(stat))


def pair_kernel(g, a1, out3, stats, message):
    refs = (g, a1)
    q, k, v, do = (join([tensor(ref, t) for ref in refs]) for t in range(4))
    more, total = attend(q, k, v)
    stat, _, added = combine(join([unpack(ref[BODY:]) for ref in refs]), total, dotted(do, more))
    out3[...] = more[:ROWS] * added[:ROWS]
    stats[0], stats[1] = stat[:ROWS], stat[ROWS:]
    message[...] = join([stat[:64], stat[ROWS : ROWS + 64]]).T[:8]


def top_kernel(g, a1, a3, a2, top):
    for t in range(4):
        top[0, t] = tensor(g, t, 32)
        top[1, t] = tensor(a1, t, 32)
        top[2, t] = a3[t, :32]
        top[3, t] = a2[t, :32]


def fours(g, a1, a3, a2):
    return [join([tensor(g, t, 64), tensor(a1, t, 64), a3[t], a2[t]]) for t in range(4)]


def spread(message):
    return join([message[...]] * 16).T


def quad_kernel(g, a1, a3, a2, out3, stats, message3, out_far, stats_far, message):
    q, k, v, do = fours(g, a1, a3, a2)
    more, total = attend(q, k, v)
    old = join([stats[0, :64], stats[1, :64], spread(message3)])
    stat, kept, added = combine(old, total, dotted(do, more))
    out_far[...] = join([out3[:64] * kept[:64] + more[:64] * added[:64], out3[64:]])
    stats_far[...] = stat
    message[...] = join([stat[64 * z : 64 * z + 32] for z in range(4)]).T[:8]


def rest_kernel(
    m0, m1, m2, m3, outs, stats, g, a1, a3, a2, out_far, stats_three, stats_far, far5, message5,
    c0, c1, c2, c3,
):
    refs = (m0, m1, m2, m3)
    own = [tensor(g, t) for t in range(4)]
    three = [join([tensor(g, t), tensor(a1, t)]) for t in range(4)]
    four = fours(g, a1, a3, a2)
    five = [
        join([four[t][64 * z : 64 * z + 32] for z in range(4)] + [far5[z, t] for z in range(4)])
        for t in range(4)
    ]
    more, total = attend(*five[:3])
    old = join([stats_far[64 * z : 64 * z + 32] for z in range(4)] + [spread(message5)])
    stat5, kept, added = combine(old, total, dotted(five[3], more))
    stat4 = join(
        [
            rows
            for z in range(4)
            for rows in (stat5[32 * z : 32 * z + 32], stats_far[64 * z + 32 : 64 * z + 64])
        ]
    )
    stat3 = join(
        [rows for z in range(2) for rows in (stat4[64 * z : 64 * z + 64], stats_three[z, 64:])]
    )
    own_stat = stat3[:ROWS]
    out = join([out_far[:32] * kept[:32] + more[:32] * added[:32], out_far[32:]])
    near = group([stats[chip] for chip in range(4)])
    out = out + group([outs[chip] for chip in range(4)]) * jnp.exp(
        total_of(near) - total_of(own_stat)
    )
    dq = dk = dv = None
    for level, (rows, gathered, stat) in enumerate(
        ((128, three, stat3), (64, four, stat4), (32, five, stat5))
    ):
        _, score = score_parts(
            own[0][:rows], gathered[1], gathered[2], own[3][:rows], own_stat[:rows]
        )
        queries = nn(score, gathered[1])
        chance, score = score_parts(
            gathered[0], own[1][:rows], own[2][:rows], gathered[3], stat
        )
        keys, values = tn(score, gathered[0]), tn(chance, gathered[3])
        if level == 0:
            dq, dk, dv = queries, keys, values
        else:
            dq, dk, dv = (
                join([whole[:rows] + part, whole[rows:]])
                for whole, part in ((dq, queries), (dk, keys), (dv, values))
            )
    stat = [join([ungroup(own_stat, chip), stats[chip, 32:]]) for chip in range(4)]
    sums = [None] * 4
    for pair in (0, 2):
        q, k, v, do = (join([tensor(refs[pair], t), tensor(refs[pair + 1], t)]) for t in range(4))
        chance, score = score_parts(q, k, v, do, join(stat[pair : pair + 2]))
        parts = nn(score, k), tn(score, q), tn(chance, do)
        for chip in range(2):
            sums[pair + chip] = [part[chip * ROWS : (chip + 1) * ROWS] for part in parts]
    q, k, v, do = (join([tensor(ref, t, 64) for ref in refs]) for t in range(4))
    chance, score = score_parts(q, k, v, do, join([s[:64] for s in stat]))
    parts = nn(score, k), tn(score, q), tn(chance, do)
    for chip, message in enumerate((c0, c1, c2, c3)):
        message[:ROWS] = join([ungroup(out, chip), outs[chip, 32:]]).astype(BF16)
        for t, (whole, part, top) in enumerate(zip(sums[chip], parts, (dq, dk, dv))):
            part = part[chip * 64 : (chip + 1) * 64]
            rows = join(
                [whole[:32] + part[:32] + ungroup(top, chip), whole[32:64] + part[32:], whole[64:]]
            )
            message[(t + 1) * ROWS : (t + 2) * ROWS] = rows.astype(BF16)
        message[BODY:] = pack(stat[chip])


def finish_kernel(
    offs_left, q, k, v, do, theirs, outs, stats, c0, c1, c2, c3, mine_out, theirs_out,
    work, offs, sem,
):
    copy = pltpu.make_async_copy(offs_left, offs, sem.at[0])
    copy.start()
    copy.wait()
    for step, message in enumerate((c0, c1, c2, c3)):
        places = chosen(offs, own_head(step))
        tensors = chip_rows(step, (q, k, v, do), theirs)
        work[step, 4] = stats[step]
        final = unpack(message[BODY:])
        for begin, rows in places:
            work[step, 4, rows, :] = final[begin : begin + rows.size]
        stat = work[step, 4]
        work[step, 0] = outs[step] * jnp.exp(total_of(stats[step]) - total_of(stat))
        chance, score = score_parts(*tensors, stat)
        work[step, 1] = nn(score, tensors[1])
        work[step, 2] = tn(score, tensors[0])
        work[step, 3] = tn(chance, tensors[3])
        for t in range(4):
            part = tensor(message, t).astype(F32)
            for begin, rows in places:
                work[step, t, rows, :] = work[step, t, rows, :] + part[begin : begin + rows.size]
            mine_out[step, t] = work[step, t, :ROWS].astype(BF16)
            theirs_out[step, t] = work[step, t, ROWS:].astype(BF16)


def place_kernel(mine, theirs, att, dq, dk, dv, rows, sems):
    copies = [
        pltpu.make_async_copy(rows.at[t], ref, sems.at[t])
        for t, ref in enumerate((att, dq, dk, dv))
    ]
    for t in range(4):
        for step in range(CHIPS):
            rows[t, :, lanes(own_head(step))] = mine[step, t]
            rows[t, :, lanes(other_head(step))] = theirs[step, t]
        copies[t].start()
    for copy in copies:
        copy.wait()


VMEM = pl.BlockSpec(memory_space=pltpu.VMEM)
LEFT = pl.BlockSpec(memory_space=pltpu.HBM)


def call(kernel, name, outs, *args, left=0, scratch=(), out_specs=None):
    stay = [pltpu.with_memory_space_constraint(arg, pltpu.HBM) for arg in args[:left]]
    args = (*stay, *args[left:])
    return pl.pallas_call(
        kernel,
        name=name,
        out_shape=tuple(jax.ShapeDtypeStruct(shape, dtype) for shape, dtype in outs),
        in_specs=[LEFT] * left + [VMEM] * (len(args) - left),
        out_specs=out_specs or (VMEM,) * len(outs),
        scratch_shapes=scratch,
        compiler_params=pltpu.CompilerParams(vmem_limit_bytes=40 * 2**20),
    )(*args)


def in_plane(array, flip):
    moves = [(PLANE * z + i, PLANE * z + (i ^ flip)) for z in range(DEPTH) for i in range(PLANE)]
    return lax.ppermute(array, "ctx", moves)


def across(array, flip):
    moves = [(PLANE * z + i, PLANE * (z ^ flip) + i) for z in range(DEPTH) for i in range(PLANE)]
    return lax.ppermute(array, "ctx", moves)


def shards(queries, keys, values, out_grad, offsets):
    whole = ((ROWS, HEADS * WIDTH), BF16)
    half = ((CHIPS, 4, ROWS, WIDTH), BF16)
    message = ((MESSAGE, WIDTH), BF16)
    flat = ((8, WIDTH), F32)
    rows = ((ROWS, WIDTH), F32)
    quads = ((4, ROWS, WIDTH), F32)
    chips = ((CHIPS, CHIP, WIDTH), F32)
    fetched = [pltpu.SMEM((6, HEADS), jnp.int32), pltpu.SemaphoreType.DMA((1,))]
    work = [pltpu.VMEM((CHIPS, 5, CHIP, WIDTH), F32)] + fetched
    *raw, theirs = call(
        split_kernel, "split", [whole] * 4 + [half], queries, keys, values, out_grad,
        left=4, scratch=[pltpu.SemaphoreType.DMA((4,))],
    )
    theirs = in_plane(theirs, 1)
    *sent, outs0, stats0 = call(
        chip_kernel, "chip", [message] * 4 + [chips] * 2, offsets, *raw, theirs,
        left=1, scratch=work,
    )
    got = [sent[0]] + [in_plane(sent[step], 2 * step) for step in (1, 2, 3)]
    outs, stats, g, g4 = call(
        near_kernel, "near", [quads, quads, message, ((4, 64, WIDTH), BF16)], *got
    )
    a1 = across(g, 1)
    a3 = across(g4, 3)
    a2 = across(g4, 2)
    out3, stats3, message3 = call(
        pair_kernel, "pair", [rows, ((2, ROWS, WIDTH), F32), flat], g, a1
    )
    a3, a2, message3 = lax.optimization_barrier((a3, a2, across(message3, 3)))
    fars = (g, a1, a3, a2)
    (top,) = call(top_kernel, "top", [((4, 4, 32, WIDTH), BF16)], *fars)
    top = across(top, 7)
    out_far, stats_far, message5 = call(
        quad_kernel, "quad", [rows, ((SEG, WIDTH), F32), flat], *fars, out3, stats3, message3
    )
    message5 = across(message5, 7)
    back = call(
        rest_kernel, "rest", [message] * 4,
        *got, outs, stats, *fars, out_far, stats3, stats_far, top, message5,
    )
    back = [back[0]] + [in_plane(back[step], 2 * step) for step in (1, 2, 3)]
    mine, theirs = call(
        finish_kernel, "finish", [half, half], offsets, *raw, theirs, outs0, stats0, *back,
        left=1, scratch=work,
    )
    theirs = in_plane(theirs, 1)
    return call(
        place_kernel, "place", [whole] * 4, mine, theirs, out_specs=(LEFT,) * 4,
        scratch=[pltpu.VMEM((4, ROWS, HEADS * WIDTH), BF16), pltpu.SemaphoreType.DMA((4,))],
    )


def solution(mesh):
    rows = P(("dp", "ctx"), None)
    return jax.shard_map(
        shards,
        mesh=mesh,
        in_specs=(rows,) * 4 + (P("dp", None),),
        out_specs=(rows,) * 4,
        check_vma=False,
    )
```

```python
import functools
import math

import jax
import jax.numpy as jnp
from jax import lax
from jax.experimental import pallas as pl
from jax.experimental.pallas import tpu as pltpu
from jax.sharding import PartitionSpec as P

HEADS = 8
WIDTH = 128
ROWS = 128
CHIP = 2 * ROWS
CHIPS = 4
PLANE = 2 * CHIPS
DEPTH = 8
SEG = 256
BODY = 4 * ROWS
MESSAGE = BODY + 32
SCALE = 1.0 / math.sqrt(WIDTH)
F32 = jnp.float32
BF16 = jnp.bfloat16


def nt(a, b):
    return lax.dot_general(a, b, (((1,), (1,)), ((), ())), preferred_element_type=F32)


def nn(a, b):
    return lax.dot_general(a, b, (((1,), (0,)), ((), ())), preferred_element_type=F32)


def tn(a, b):
    return lax.dot_general(a, b, (((0,), (0,)), ((), ())), preferred_element_type=F32)


def join(parts):
    return jnp.concatenate(parts, axis=0)


def attend(*blocks):
    scores = [nt(q, k) * SCALE for q, k, _ in blocks]
    peaks = [jnp.max(s, axis=1, keepdims=True) for s in scores]
    grown = [jnp.exp(s - peak) for s, peak in zip(scores, peaks)]
    masses = [jnp.sum(g, axis=1, keepdims=True) for g in grown]
    weights = [(g * (1.0 / mass)).astype(BF16) for g, mass in zip(grown, masses)]
    outs = [nn(w, v) for w, (_, _, v) in zip(weights, blocks)]
    return [(o, wide(peak + jnp.log(mass))) for o, peak, mass in zip(outs, peaks, masses)]


def dotted(a, b):
    return wide(jnp.sum(a.astype(F32) * b, axis=1, keepdims=True))


def wide(column):
    return jnp.broadcast_to(column, (column.shape[0], WIDTH))


def across_lanes(column):
    return jnp.concatenate([column, column], axis=1)


def rows_of(stat, begin, end):
    return [column[begin:end] for column in stat]


def stack(stats):
    return [join([stat[i] for stat in stats]) for i in range(2)]


def combine(stat, total, delta):
    peak = jnp.maximum(stat[0], total)
    kept, added = jnp.exp(stat[0] - peak), jnp.exp(total - peak)
    mass = kept + added
    share = 1.0 / mass
    kept, added = kept * share, added * share
    return [peak + jnp.log(mass), kept * stat[1] + added * delta], kept, added


def flatten(stat):
    lane = lax.broadcasted_iota(jnp.int32, (1, WIDTH), 1)
    return jnp.where(lane & 4 == 0, stat[0], stat[1]).T[:8]


def unflatten(flat):
    return [jnp.broadcast_to(flat[i : i + 1], (WIDTH, flat.shape[1])).T for i in (0, 4)]


def three_terms(values):
    high = values.astype(BF16).astype(F32)
    middle = (values - high).astype(BF16).astype(F32)
    return [term.astype(BF16) for term in (high, middle, values - high - middle)]


def pack(stat):
    flat = flatten(stat)
    return join([term.astype(F32) for term in three_terms(flat)] + [jnp.zeros_like(flat)]).astype(BF16)


def unpack(rows):
    terms = rows.astype(F32)
    return unflatten(terms[:8] + terms[8:16] + terms[16:24])


def products(blocks):
    return [nt(q, k) for q, k, _, _ in blocks], [nt(do, v) for _, _, v, do in blocks]


def fit(column, columns):
    return across_lanes(column) if columns == SEG else column[:, :columns]


def scored(scores, grads, stats):
    chances = [
        jnp.exp(s * SCALE - fit(stat[0], s.shape[1])) for s, stat in zip(scores, stats)
    ]
    parts = [
        (chance * (grad - fit(stat[1], grad.shape[1])) * SCALE).astype(BF16)
        for chance, grad, stat in zip(chances, grads, stats)
    ]
    return [(chance.astype(BF16), part) for chance, part in zip(chances, parts)]


def position(offs, head, i):
    place = (offs[2, head] ^ 2) + 4 * (i - 64)
    for below, level, flip, begin in ((64, 3, 4, 32), (32, 4, 8, 16), (16, 5, 16, 8), (8, 5, 0, 0)):
        stride = 32 if level == 5 else 2**level
        place = jnp.where(i < below, (offs[level, head] ^ flip) + stride * (i - begin), place)
    return place


def picking(offs, head):
    i = lax.broadcasted_iota(jnp.int32, (ROWS, WIDTH), 0)
    lane = lax.broadcasted_iota(jnp.int32, (ROWS, WIDTH), 1)
    place = position(offs, head, i)
    hits = [jnp.where(place == lane + begin, 1.0, 0.0).astype(BF16) for begin in (0, WIDTH)]
    return jnp.concatenate(hits, axis=1)


def placing(offs, head):
    place = position(offs, head, lax.broadcasted_iota(jnp.int32, (1, WIDTH), 1))
    row = lax.broadcasted_iota(jnp.int32, (CHIP, WIDTH), 0)
    return jnp.where(row == place, 1.0, 0.0).astype(BF16)


def side_by_side(parts):
    return jnp.concatenate(parts, axis=1)


def lanes(head):
    return pl.ds(pl.multiple_of(head * WIDTH, WIDTH), WIDTH)


def own_head(step):
    spot = lax.axis_index("ctx") % PLANE
    return spot ^ (2 * step)


def other_head(step):
    return own_head(step) ^ 1


def split_kernel(q, k, v, do, q_in, k_in, v_in, do_in, theirs, sems):
    inside = (q_in, k_in, v_in, do_in)
    copies = [
        pltpu.make_async_copy(ref, to, sems.at[t])
        for t, (ref, to) in enumerate(zip((q, k, v, do), inside))
    ]
    for copy in copies:
        copy.start()
    for t, ref in enumerate(inside):
        copies[t].wait()
        for step in range(CHIPS):
            theirs[step, t] = ref[:, lanes(other_head(step))]


def chip_rows(step, raw, theirs):
    head = own_head(step)
    return [join([ref[:, lanes(head)], theirs[step, t]]) for t, ref in enumerate(raw)]


def maps_kernel(offs_left, picks, places, offs, sem):
    copy = pltpu.make_async_copy(offs_left, offs, sem.at[0])
    copy.start()
    copy.wait()
    for step in range(CHIPS):
        picks[step] = picking(offs, own_head(step))
        places[step] = placing(offs, own_head(step))


def chip_kernel(q, k, v, do, theirs, picks, m0, m1, m2, m3, outs, stats):
    messages = (m0, m1, m2, m3)
    tensors = [chip_rows(step, (q, k, v, do), theirs) for step in range(CHIPS)]
    found = attend(*(rows[:3] for rows in tensors))
    picked = [nn(picks[step], side_by_side(tensors[step])) for step in range(CHIPS)]
    deltas = [dotted(tensors[step][3], found[step][0]) for step in range(CHIPS)]
    for step, message in enumerate(messages):
        for t in range(4):
            rows = picked[step][:, t * WIDTH : (t + 1) * WIDTH]
            message[t * ROWS : (t + 1) * ROWS] = rows.astype(BF16)
    lane = lax.broadcasted_iota(jnp.int32, (1, WIDTH), 1)
    for step, message in enumerate(messages):
        out, total = found[step]
        outs[step] = out
        stats[step, 0] = total
        stats[step, 1] = deltas[step]
        flat = jnp.where(lane & 4 == 0, total, deltas[step]).T[:8]
        flat = nt(join([term.astype(F32) for term in three_terms(flat)]).astype(BF16), picks[step])
        message[BODY:] = join([flat, jnp.zeros((8, WIDTH), F32)]).astype(BF16)


def alone_kernel(places, stats, others):
    for step in range(CHIPS):
        alone = 1.0 - nn(places[step], jnp.ones((ROWS, WIDTH), BF16))
        for i in range(2):
            others[step, i] = stats[step, i] * alone


def tensor(ref, t, rows=ROWS):
    return ref[t * ROWS : t * ROWS + rows]


def group(parts):
    return join(
        [p[:8] for p in parts] + [p[8:16] for p in parts] + [p[16:32] for p in parts]
    )


def ungroup(rows, chip):
    return join(
        [
            rows[8 * chip : 8 * chip + 8],
            rows[32 + 8 * chip : 40 + 8 * chip],
            rows[64 + 16 * chip : 80 + 16 * chip],
        ]
    )


def near_kernel(m0, m1, m2, m3, outs, stats, g, g4):
    refs = (m0, m1, m2, m3)
    stat = [unpack(ref[BODY:]) for ref in refs]
    out = [None] * 4
    blocks = [
        [join([tensor(refs[pair], t), tensor(refs[pair + 1], t)]) for t in range(4)]
        for pair in (0, 2)
    ]
    blocks.append([join([tensor(ref, t, 64) for ref in refs]) for t in range(4)])
    found = attend(*(block[:3] for block in blocks))
    deltas = [dotted(block[3], more) for block, (more, _) in zip(blocks, found)]
    for pair in (0, 2):
        more, total = found[pair // 2]
        joined, _, added = combine(stack(stat[pair : pair + 2]), total, deltas[pair // 2])
        more = more * added
        for chip in range(2):
            out[pair + chip] = more[chip * ROWS : (chip + 1) * ROWS]
            stat[pair + chip] = rows_of(joined, chip * ROWS, (chip + 1) * ROWS)
    more, total = found[2]
    joined, kept, added = combine(stack([rows_of(s, 0, 64) for s in stat]), total, deltas[2])
    more = join([o[:64] for o in out]) * kept + more * added
    for chip in range(4):
        out[chip] = join([more[chip * 64 : (chip + 1) * 64], out[chip][64:]])
        stat[chip] = stack(
            [rows_of(joined, chip * 64, (chip + 1) * 64), rows_of(stat[chip], 64, ROWS)]
        )
        outs[chip] = out[chip]
        stats[chip, 0], stats[chip, 1] = stat[chip]
    for t in range(4):
        rows = group([tensor(ref, t, 32).astype(F32) for ref in refs])
        rows = rows.astype(BF16)
        g[t * ROWS : (t + 1) * ROWS] = rows
        g4[t] = rows[:64]
    g[BODY:] = pack([group([s[i] for s in stat]) for i in range(2)])


def below_kernel(m0, m1, m2, m3, stats, sums):
    refs = (m0, m1, m2, m3)
    stat = [[stats[chip, i] for i in range(2)] for chip in range(4)]
    tensors = [[tensor(ref, t) for t in range(4)] for ref in refs]
    blocks, block_stats = [], []
    for pair in (0, 2):
        k, v = (join([tensors[pair][t], tensors[pair + 1][t]]) for t in (1, 2))
        q, do = (join([tensors[pair][t][32:], tensors[pair + 1][t][32:]]) for t in (0, 3))
        blocks.append((q, k, v, do))
        block_stats.append(stack([rows_of(s, 32, ROWS) for s in stat[pair : pair + 2]]))
    k, v = (join([rows[t][:64] for rows in tensors]) for t in (1, 2))
    q, do = (join([rows[t][32:64] for rows in tensors]) for t in (0, 3))
    blocks.append((q, k, v, do))
    block_stats.append(stack([rows_of(s, 32, 64) for s in stat]))
    found = scored(*products(blocks), block_stats)
    dqs = [nn(score, block[1]) for (_, score), block in zip(found, blocks)]
    dks = [tn(score, block[0]) for (_, score), block in zip(found, blocks)]
    dvs = [tn(chance, block[3]) for (chance, _), block in zip(found, blocks)]
    whole = [
        [
            dqs[chip // 2][chip % 2 * 96 : chip % 2 * 96 + 96],
            dks[chip // 2][chip % 2 * ROWS : chip % 2 * ROWS + ROWS],
            dvs[chip // 2][chip % 2 * ROWS : chip % 2 * ROWS + ROWS],
        ]
        for chip in range(4)
    ]
    parts = dqs[2], dks[2], dvs[2]
    for chip in range(4):
        sums[chip, 0, :32] = jnp.zeros((32, WIDTH), F32)
        sums[chip, 0, 32:64] = whole[chip][0][:32] + parts[0][chip * 32 : (chip + 1) * 32]
        sums[chip, 0, 64:] = whole[chip][0][32:]
        for i in (1, 2):
            sums[chip, i, :64] = whole[chip][i][:64] + parts[i][chip * 64 : (chip + 1) * 64]
            sums[chip, i, 64:] = whole[chip][i][64:]


def pair_kernel(g, a1, out3, stats, message):
    refs = (g, a1)
    q, k, v, do = (join([tensor(ref, t) for ref in refs]) for t in range(4))
    ((more, total),) = attend((q, k, v))
    stat, _, added = combine(stack([unpack(ref[BODY:]) for ref in refs]), total, dotted(do, more))
    out3[...] = more[:ROWS] * added[:ROWS]
    stats[0], stats[1] = stat
    message[...] = flatten(stack([rows_of(stat, 0, 64), rows_of(stat, ROWS, ROWS + 64)]))


def top_kernel(g, a1, a3, a2, top):
    for t in range(4):
        top[0, t] = tensor(g, t, 32)
        top[1, t] = tensor(a1, t, 32)
        top[2, t] = a3[t, :32]
        top[3, t] = a2[t, :32]


def fours(g, a1, a3, a2):
    return [join([tensor(g, t, 64), tensor(a1, t, 64), a3[t], a2[t]]) for t in range(4)]


def quad_kernel(g, a1, a3, a2, out3, stats, message3, out_far, stats_far, message):
    q, k, v, do = fours(g, a1, a3, a2)
    ((more, total),) = attend((q, k, v))
    old = [join([stats[i, :64], stats[i, ROWS : ROWS + 64]]) for i in range(2)]
    old = stack([old, unflatten(message3[...])])
    stat, kept, added = combine(old, total, dotted(do, more))
    out_far[...] = join([out3[:64] * kept[:64] + more[:64] * added[:64], out3[64:]])
    stats_far[0], stats_far[1] = stat
    message[...] = flatten(stack([rows_of(stat, 64 * z, 64 * z + 32) for z in range(4)]))


def rest_kernel(
    m0, m1, m2, m3, outs, stats, below, g, a1, a3, a2, out_far, stats_three, stats_far, far5,
    message5, c0, c1, c2, c3,
):
    refs = (m0, m1, m2, m3)
    own = [tensor(g, t) for t in range(4)]
    three = [join([tensor(g, t), tensor(a1, t)]) for t in range(4)]
    four = fours(g, a1, a3, a2)
    five = [
        join([four[t][64 * z : 64 * z + 32] for z in range(4)] + [far5[z, t] for z in range(4)])
        for t in range(4)
    ]
    blocks = []
    for rows, gathered in ((128, three), (64, four), (32, five)):
        mine = [part[:rows] for part in own]
        blocks.append((mine[0], gathered[1], gathered[2], mine[3]))
        blocks.append((gathered[0], mine[1], mine[2], gathered[3]))
    for pair in (0, 2):
        k, v = (join([tensor(refs[pair], t), tensor(refs[pair + 1], t)]) for t in (1, 2))
        q, do = (join([tensor(refs[pair], t, 32), tensor(refs[pair + 1], t, 32)]) for t in (0, 3))
        blocks.append((q, k, v, do))
    k, v = (join([tensor(ref, t, 64) for ref in refs]) for t in (1, 2))
    q, do = (join([tensor(ref, t, 32) for ref in refs]) for t in (0, 3))
    blocks.append((q, k, v, do))
    ((more, total),) = attend(five[:3])
    scores, grads = products(blocks)
    four_stat = [stats_far[0], stats_far[1]]
    three_stat = [stats_three[0], stats_three[1]]
    old = stack(
        [rows_of(four_stat, 64 * z, 64 * z + 32) for z in range(4)] + [unflatten(message5[...])]
    )
    stat5, kept, added = combine(old, total, dotted(five[3], more))
    stat4 = stack(
        [
            rows
            for z in range(4)
            for rows in (
                rows_of(stat5, 32 * z, 32 * z + 32),
                rows_of(four_stat, 64 * z + 32, 64 * z + 64),
            )
        ]
    )
    stat3 = stack(
        [
            rows
            for z in range(2)
            for rows in (
                rows_of(stat4, 64 * z, 64 * z + 64),
                rows_of(three_stat, ROWS * z + 64, ROWS * z + ROWS),
            )
        ]
    )
    own_stat = rows_of(stat3, 0, ROWS)
    out = join([out_far[:32] * kept[:32] + more[:32] * added[:32], out_far[32:]])
    near = group([stats[chip, 0] for chip in range(4)])
    out = out + group([outs[chip] for chip in range(4)]) * jnp.exp(near - own_stat[0])
    stat = [[ungroup(own_stat[i], chip) for i in range(2)] for chip in range(4)]
    block_stats = []
    for rows, gathered in ((128, stat3), (64, stat4), (32, stat5)):
        block_stats += [rows_of(own_stat, 0, rows), gathered]
    block_stats += [stack(stat[:2]), stack(stat[2:]), stack(stat)]
    found = scored(scores, grads, block_stats)
    dqs = [nn(found[i][1], blocks[i][1]) for i in (0, 2, 4, 6, 7, 8)]
    dks = [tn(found[i][1], blocks[i][0]) for i in (1, 3, 5, 6, 7, 8)]
    dvs = [tn(found[i][0], blocks[i][3]) for i in (1, 3, 5, 6, 7, 8)]
    dq, dk, dv = (
        join([f[:32] + g[:32] + h, f[32:64] + g[32:], f[64:]]) for f, g, h, *_ in (dqs, dks, dvs)
    )
    sums = [
        [
            dqs[3 + chip // 2][chip % 2 * 32 : chip % 2 * 32 + 32],
            dks[3 + chip // 2][chip % 2 * ROWS : chip % 2 * ROWS + ROWS],
            dvs[3 + chip // 2][chip % 2 * ROWS : chip % 2 * ROWS + ROWS],
        ]
        for chip in range(4)
    ]
    parts = dqs[5], dks[5], dvs[5]
    for chip, message in enumerate((c0, c1, c2, c3)):
        message[:ROWS] = join([ungroup(out, chip), outs[chip, 32:]]).astype(BF16)
        rows = sums[chip][0] + parts[0][chip * 32 : (chip + 1) * 32] + ungroup(dq, chip)
        message[ROWS : 2 * ROWS] = join([rows, below[chip, 0, 32:]]).astype(BF16)
        for i, top in ((1, dk), (2, dv)):
            whole = below[chip, i] + sums[chip][i]
            part = parts[i][chip * 64 : (chip + 1) * 64]
            rows = join([whole[:32] + part[:32] + ungroup(top, chip), whole[32:64] + part[32:], whole[64:]])
            message[(i + 1) * ROWS : (i + 2) * ROWS] = rows.astype(BF16)
        message[BODY:] = pack(
            [join([stat[chip][i], stats[chip, i, 32:]]) for i in range(2)]
        )


def finish_kernel(steps, q, k, v, do, theirs, places, outs, stats, others, c0, c1, *refs):
    mine_out, theirs_out = refs[-2:]
    messages = (c0, c1)
    tensors = [chip_rows(step, (q, k, v, do), theirs) for step in steps]
    scores, grads = products(tensors)
    terms = [nt(message[BODY:], places[step]) for step, message in zip(steps, messages)]
    finals = [unflatten(rows[:8] + rows[8:16] + rows[16:24]) for rows in terms]
    stat = [[others[step, i] + final[i] for i in range(2)] for step, final in zip(steps, finals)]
    back = [
        nn(places[step], side_by_side([tensor(message, t) for t in range(4)]))
        for step, message in zip(steps, messages)
    ]
    found = scored(scores, grads, stat)
    own = [
        [outs[step] * jnp.exp(stats[step, 0] - stat[slot][0]) for slot, step in enumerate(steps)],
        [nn(score, rows[1]) for (_, score), rows in zip(found, tensors)],
        [tn(score, rows[0]) for (_, score), rows in zip(found, tensors)],
        [tn(chance, rows[3]) for (chance, _), rows in zip(found, tensors)],
    ]
    for slot in range(2):
        for t in range(4):
            rows = own[t][slot] + back[slot][:, t * WIDTH : (t + 1) * WIDTH]
            mine_out[slot, t] = rows[:ROWS].astype(BF16)
            theirs_out[slot, t] = rows[ROWS:].astype(BF16)


def place_kernel(mine0, mine1, theirs0, theirs1, att, dq, dk, dv, rows, sems):
    copies = [
        pltpu.make_async_copy(rows.at[t], ref, sems.at[t])
        for t, ref in enumerate((att, dq, dk, dv))
    ]
    for t in range(4):
        for step in range(CHIPS):
            mine, theirs = ((mine0, theirs0), (mine1, theirs1))[step // 2]
            rows[t, :, lanes(own_head(step))] = mine[step % 2, t]
            rows[t, :, lanes(other_head(step))] = theirs[step % 2, t]
        copies[t].start()
    for copy in copies:
        copy.wait()


VMEM = pl.BlockSpec(memory_space=pltpu.VMEM)
LEFT = pl.BlockSpec(memory_space=pltpu.HBM)


def call(kernel, name, outs, *args, left=0, scratch=(), out_specs=None):
    stay = [pltpu.with_memory_space_constraint(arg, pltpu.HBM) for arg in args[:left]]
    args = (*stay, *args[left:])
    return pl.pallas_call(
        kernel,
        name=name,
        out_shape=tuple(jax.ShapeDtypeStruct(shape, dtype) for shape, dtype in outs),
        in_specs=[LEFT] * left + [VMEM] * (len(args) - left),
        out_specs=out_specs or (VMEM,) * len(outs),
        scratch_shapes=scratch,
        compiler_params=pltpu.CompilerParams(vmem_limit_bytes=40 * 2**20),
    )(*args)


def in_plane(array, flip):
    moves = [(PLANE * z + i, PLANE * z + (i ^ flip)) for z in range(DEPTH) for i in range(PLANE)]
    return lax.ppermute(array, "ctx", moves)


def across(array, flip):
    moves = [(PLANE * z + i, PLANE * (z ^ flip) + i) for z in range(DEPTH) for i in range(PLANE)]
    return lax.ppermute(array, "ctx", moves)


def shards(queries, keys, values, out_grad, offsets):
    whole = ((ROWS, HEADS * WIDTH), BF16)
    half = ((CHIPS, 4, ROWS, WIDTH), BF16)
    pairs = ((2, 4, ROWS, WIDTH), BF16)
    message = ((MESSAGE, WIDTH), BF16)
    flat = ((8, WIDTH), F32)
    rows = ((ROWS, WIDTH), F32)
    quads = ((4, ROWS, WIDTH), F32)
    quad_stats = ((4, 2, ROWS, WIDTH), F32)
    chips = ((CHIPS, CHIP, WIDTH), F32)
    chip_stats = ((CHIPS, 2, CHIP, WIDTH), F32)
    seg_stats = ((2, SEG, WIDTH), F32)
    *raw, theirs = call(
        split_kernel, "split", [whole] * 4 + [half], queries, keys, values, out_grad,
        left=4, scratch=[pltpu.SemaphoreType.DMA((4,))],
    )
    theirs = in_plane(theirs, 1)
    picks, places = call(
        maps_kernel, "maps", [((CHIPS, ROWS, CHIP), BF16), ((CHIPS, CHIP, ROWS), BF16)], offsets,
        left=1, scratch=[pltpu.SMEM((6, HEADS), jnp.int32), pltpu.SemaphoreType.DMA((1,))],
    )
    *sent, outs0, stats0 = call(
        chip_kernel, "chip", [message] * 4 + [chips, chip_stats], *raw, theirs, picks
    )
    (others,) = call(alone_kernel, "alone", [chip_stats], places, stats0)
    got = [sent[0]] + [in_plane(sent[step], 2 * step) for step in (1, 2, 3)]
    outs, stats, g, g4 = call(
        near_kernel, "near", [quads, quad_stats, message, ((4, 64, WIDTH), BF16)], *got
    )
    (below,) = call(below_kernel, "below", [((4, 3, ROWS, WIDTH), F32)], *got, stats)
    a1 = across(g, 1)
    a3 = across(g4, 3)
    a2 = across(g4, 2)
    out3, stats3, message3 = call(
        pair_kernel, "pair", [rows, seg_stats, flat], g, a1
    )
    a3, a2, message3 = lax.optimization_barrier((a3, a2, across(message3, 3)))
    fars = (g, a1, a3, a2)
    (top,) = call(top_kernel, "top", [((4, 4, 32, WIDTH), BF16)], *fars)
    top = across(top, 7)
    out_far, stats_far, message5 = call(
        quad_kernel, "quad", [rows, seg_stats, flat], *fars, out3, stats3, message3
    )
    message5 = across(message5, 7)
    back = call(
        rest_kernel, "rest", [message] * 4,
        *got, outs, stats, below, *fars, out_far, stats3, stats_far, top, message5,
    )
    back = [back[0]] + [in_plane(back[step], 2 * step) for step in (1, 2, 3)]
    halves, after = [], ()
    for steps in ((0, 1), (2, 3)):
        mine, other = call(
            functools.partial(finish_kernel, steps), "finish", [pairs, pairs],
            *raw, theirs, places, outs0, stats0, others, *(back[step] for step in steps), *after,
        )
        after = (mine,)
        halves.append((mine, in_plane(other, 1)))
    (mine0, theirs0), (mine1, theirs1) = halves
    return call(
        place_kernel, "place", [whole] * 4, mine0, mine1, theirs0, theirs1, out_specs=(LEFT,) * 4,
        scratch=[pltpu.VMEM((4, ROWS, HEADS * WIDTH), BF16), pltpu.SemaphoreType.DMA((4,))],
    )


def solution(mesh):
    rows = P(("dp", "ctx"), None)
    return jax.shard_map(
        shards,
        mesh=mesh,
        in_specs=(rows,) * 4 + (P("dp", None),),
        out_specs=(rows,) * 4,
        check_vma=False,
    )
```

```python
import functools
import math

import jax
import jax.numpy as jnp
from jax import lax
from jax.experimental import pallas as pl
from jax.experimental.pallas import tpu as pltpu
from jax.sharding import PartitionSpec as P

HEADS = 8
WIDTH = 128
ROWS = 128
CHIP = 2 * ROWS
CHIPS = 4
PLANE = 2 * CHIPS
DEPTH = 8
SEG = 256
BODY = 4 * ROWS
MESSAGE = BODY + 32
SCALE = 1.0 / math.sqrt(WIDTH)
F32 = jnp.float32
BF16 = jnp.bfloat16


def nt(a, b):
    return lax.dot_general(a, b, (((1,), (1,)), ((), ())), preferred_element_type=F32)


def nn(a, b):
    return lax.dot_general(a, b, (((1,), (0,)), ((), ())), preferred_element_type=F32)


def tn(a, b):
    return lax.dot_general(a, b, (((0,), (0,)), ((), ())), preferred_element_type=F32)


def join(parts):
    return jnp.concatenate(parts, axis=0)


def attend(*blocks):
    scores = [nt(q, k) * SCALE for q, k, _ in blocks]
    peaks = [jnp.max(s, axis=1, keepdims=True) for s in scores]
    grown = [jnp.exp(s - peak) for s, peak in zip(scores, peaks)]
    masses = [jnp.sum(g, axis=1, keepdims=True) for g in grown]
    weights = [(g * (1.0 / mass)).astype(BF16) for g, mass in zip(grown, masses)]
    outs = [nn(w, v) for w, (_, _, v) in zip(weights, blocks)]
    return [(o, wide(peak + jnp.log(mass))) for o, peak, mass in zip(outs, peaks, masses)]


def dotted(a, b):
    return wide(jnp.sum(a.astype(F32) * b, axis=1, keepdims=True))


def wide(column):
    return jnp.broadcast_to(column, (column.shape[0], WIDTH))


def across_lanes(column):
    return jnp.concatenate([column, column], axis=1)


def rows_of(stat, begin, end):
    return [column[begin:end] for column in stat]


def stack(stats):
    return [join([stat[i] for stat in stats]) for i in range(2)]


def combine(stat, total, delta):
    peak = jnp.maximum(stat[0], total)
    kept, added = jnp.exp(stat[0] - peak), jnp.exp(total - peak)
    mass = kept + added
    share = 1.0 / mass
    kept, added = kept * share, added * share
    return [peak + jnp.log(mass), kept * stat[1] + added * delta], kept, added


def flatten(stat):
    lane = lax.broadcasted_iota(jnp.int32, (1, WIDTH), 1)
    return jnp.where(lane & 4 == 0, stat[0], stat[1]).T[:8]


def unflatten(flat):
    return [jnp.broadcast_to(flat[i : i + 1], (WIDTH, flat.shape[1])).T for i in (0, 4)]


def three_terms(values):
    high = values.astype(BF16).astype(F32)
    middle = (values - high).astype(BF16).astype(F32)
    return [term.astype(BF16) for term in (high, middle, values - high - middle)]


def pack(stat):
    flat = flatten(stat)
    return join([term.astype(F32) for term in three_terms(flat)] + [jnp.zeros_like(flat)]).astype(BF16)


def unpack(rows):
    terms = rows.astype(F32)
    return unflatten(terms[:8] + terms[8:16] + terms[16:24])


def products(blocks):
    return [nt(q, k) for q, k, _, _ in blocks], [nt(do, v) for _, _, v, do in blocks]


def fit(column, columns):
    return across_lanes(column) if columns == SEG else column[:, :columns]


def scored(scores, grads, stats):
    chances = [
        jnp.exp(s * SCALE - fit(stat[0], s.shape[1])) for s, stat in zip(scores, stats)
    ]
    parts = [
        (chance * (grad - fit(stat[1], grad.shape[1])) * SCALE).astype(BF16)
        for chance, grad, stat in zip(chances, grads, stats)
    ]
    return [(chance.astype(BF16), part) for chance, part in zip(chances, parts)]


def position(offs, head, i):
    place = (offs[2, head] ^ 2) + 4 * (i - 64)
    for below, level, flip, begin in ((64, 3, 4, 32), (32, 4, 8, 16), (16, 5, 16, 8), (8, 5, 0, 0)):
        stride = 32 if level == 5 else 2**level
        place = jnp.where(i < below, (offs[level, head] ^ flip) + stride * (i - begin), place)
    return place


def picking(offs, head):
    i = lax.broadcasted_iota(jnp.int32, (ROWS, WIDTH), 0)
    lane = lax.broadcasted_iota(jnp.int32, (ROWS, WIDTH), 1)
    place = position(offs, head, i)
    hits = [jnp.where(place == lane + begin, 1.0, 0.0).astype(BF16) for begin in (0, WIDTH)]
    return jnp.concatenate(hits, axis=1)


def placing(offs, head):
    place = position(offs, head, lax.broadcasted_iota(jnp.int32, (1, WIDTH), 1))
    row = lax.broadcasted_iota(jnp.int32, (CHIP, WIDTH), 0)
    return jnp.where(row == place, 1.0, 0.0).astype(BF16)


def side_by_side(parts):
    return jnp.concatenate(parts, axis=1)


def lanes(head):
    return pl.ds(pl.multiple_of(head * WIDTH, WIDTH), WIDTH)


def own_head(step):
    spot = lax.axis_index("ctx") % PLANE
    return spot ^ (2 * step)


def other_head(step):
    return own_head(step) ^ 1


def split_kernel(q, k, v, do, q_in, k_in, v_in, do_in, theirs, sems):
    inside = (q_in, k_in, v_in, do_in)
    copies = [
        pltpu.make_async_copy(ref, to, sems.at[t])
        for t, (ref, to) in enumerate(zip((q, k, v, do), inside))
    ]
    for copy in copies:
        copy.start()
    for t, ref in enumerate(inside):
        copies[t].wait()
        for step in range(CHIPS):
            theirs[step, t] = ref[:, lanes(other_head(step))]


def chip_rows(step, raw, theirs):
    head = own_head(step)
    return [join([ref[:, lanes(head)], theirs[step, t]]) for t, ref in enumerate(raw)]


def maps_kernel(offs_left, picks, places, offs, sem):
    copy = pltpu.make_async_copy(offs_left, offs, sem.at[0])
    copy.start()
    copy.wait()
    for step in range(CHIPS):
        picks[step] = picking(offs, own_head(step))
        places[step] = placing(offs, own_head(step))


def chip_kernel(q, k, v, do, theirs, picks, m0, m1, m2, m3, outs, stats):
    messages = (m0, m1, m2, m3)
    tensors = [chip_rows(step, (q, k, v, do), theirs) for step in range(CHIPS)]
    found = attend(*(rows[:3] for rows in tensors))
    picked = [nn(picks[step], side_by_side(tensors[step])) for step in range(CHIPS)]
    deltas = [dotted(tensors[step][3], found[step][0]) for step in range(CHIPS)]
    for step, message in enumerate(messages):
        for t in range(4):
            rows = picked[step][:, t * WIDTH : (t + 1) * WIDTH]
            message[t * ROWS : (t + 1) * ROWS] = rows.astype(BF16)
    lane = lax.broadcasted_iota(jnp.int32, (1, WIDTH), 1)
    for step, message in enumerate(messages):
        out, total = found[step]
        outs[step] = out
        stats[step, 0] = total
        stats[step, 1] = deltas[step]
        flat = jnp.where(lane & 4 == 0, total, deltas[step]).T[:8]
        flat = nt(join([term.astype(F32) for term in three_terms(flat)]).astype(BF16), picks[step])
        message[BODY:] = join([flat, jnp.zeros((8, WIDTH), F32)]).astype(BF16)


def alone_kernel(places, stats, others):
    for step in range(CHIPS):
        alone = 1.0 - nn(places[step], jnp.ones((ROWS, WIDTH), BF16))
        for i in range(2):
            others[step, i] = stats[step, i] * alone


def tensor(ref, t, rows=ROWS):
    return ref[t * ROWS : t * ROWS + rows]


def group(parts):
    return join(
        [p[:8] for p in parts] + [p[8:16] for p in parts] + [p[16:32] for p in parts]
    )


def ungroup(rows, chip):
    return join(
        [
            rows[8 * chip : 8 * chip + 8],
            rows[32 + 8 * chip : 40 + 8 * chip],
            rows[64 + 16 * chip : 80 + 16 * chip],
        ]
    )


def near_kernel(m0, m1, m2, m3, outs, stats, g, g4):
    refs = (m0, m1, m2, m3)
    stat = [unpack(ref[BODY:]) for ref in refs]
    out = [None] * 4
    blocks = [
        [join([tensor(refs[pair], t), tensor(refs[pair + 1], t)]) for t in range(4)]
        for pair in (0, 2)
    ]
    blocks.append([join([tensor(ref, t, 64) for ref in refs]) for t in range(4)])
    found = attend(*(block[:3] for block in blocks))
    deltas = [dotted(block[3], more) for block, (more, _) in zip(blocks, found)]
    for pair in (0, 2):
        more, total = found[pair // 2]
        joined, _, added = combine(stack(stat[pair : pair + 2]), total, deltas[pair // 2])
        more = more * added
        for chip in range(2):
            out[pair + chip] = more[chip * ROWS : (chip + 1) * ROWS]
            stat[pair + chip] = rows_of(joined, chip * ROWS, (chip + 1) * ROWS)
    more, total = found[2]
    joined, kept, added = combine(stack([rows_of(s, 0, 64) for s in stat]), total, deltas[2])
    more = join([o[:64] for o in out]) * kept + more * added
    for chip in range(4):
        out[chip] = join([more[chip * 64 : (chip + 1) * 64], out[chip][64:]])
        stat[chip] = stack(
            [rows_of(joined, chip * 64, (chip + 1) * 64), rows_of(stat[chip], 64, ROWS)]
        )
        outs[chip] = out[chip]
        stats[chip, 0], stats[chip, 1] = stat[chip]
    for t in range(4):
        rows = group([tensor(ref, t, 32).astype(F32) for ref in refs])
        rows = rows.astype(BF16)
        g[t * ROWS : (t + 1) * ROWS] = rows
        g4[t] = rows[:64]
    g[BODY:] = pack([group([s[i] for s in stat]) for i in range(2)])


def below_kernel(m0, m1, m2, m3, stats, sums):
    refs = (m0, m1, m2, m3)
    stat = [[stats[chip, i] for i in range(2)] for chip in range(4)]
    tensors = [[tensor(ref, t) for t in range(4)] for ref in refs]
    blocks, block_stats = [], []
    for pair in (0, 2):
        k, v = (join([tensors[pair][t], tensors[pair + 1][t]]) for t in (1, 2))
        q, do = (join([tensors[pair][t][32:], tensors[pair + 1][t][32:]]) for t in (0, 3))
        blocks.append((q, k, v, do))
        block_stats.append(stack([rows_of(s, 32, ROWS) for s in stat[pair : pair + 2]]))
    k, v = (join([rows[t][:64] for rows in tensors]) for t in (1, 2))
    q, do = (join([rows[t][32:64] for rows in tensors]) for t in (0, 3))
    blocks.append((q, k, v, do))
    block_stats.append(stack([rows_of(s, 32, 64) for s in stat]))
    found = scored(*products(blocks), block_stats)
    dqs = [nn(score, block[1]) for (_, score), block in zip(found, blocks)]
    dks = [tn(score, block[0]) for (_, score), block in zip(found, blocks)]
    dvs = [tn(chance, block[3]) for (chance, _), block in zip(found, blocks)]
    whole = [
        [
            dqs[chip // 2][chip % 2 * 96 : chip % 2 * 96 + 96],
            dks[chip // 2][chip % 2 * ROWS : chip % 2 * ROWS + ROWS],
            dvs[chip // 2][chip % 2 * ROWS : chip % 2 * ROWS + ROWS],
        ]
        for chip in range(4)
    ]
    parts = dqs[2], dks[2], dvs[2]
    for chip in range(4):
        sums[chip, 0, :32] = jnp.zeros((32, WIDTH), F32)
        sums[chip, 0, 32:64] = whole[chip][0][:32] + parts[0][chip * 32 : (chip + 1) * 32]
        sums[chip, 0, 64:] = whole[chip][0][32:]
        for i in (1, 2):
            sums[chip, i, :64] = whole[chip][i][:64] + parts[i][chip * 64 : (chip + 1) * 64]
            sums[chip, i, 64:] = whole[chip][i][64:]


def pair_kernel(g, a1, out3, stats, message):
    refs = (g, a1)
    q, k, v, do = (join([tensor(ref, t) for ref in refs]) for t in range(4))
    ((more, total),) = attend((q, k, v))
    stat, _, added = combine(stack([unpack(ref[BODY:]) for ref in refs]), total, dotted(do, more))
    out3[...] = more[:ROWS] * added[:ROWS]
    stats[0], stats[1] = stat
    message[...] = flatten(stack([rows_of(stat, 0, 64), rows_of(stat, ROWS, ROWS + 64)]))


def top_kernel(g, a1, a3, a2, top):
    for t in range(4):
        top[0, t] = tensor(g, t, 32)
        top[1, t] = tensor(a1, t, 32)
        top[2, t] = a3[t, :32]
        top[3, t] = a2[t, :32]


def fours(g, a1, a3, a2):
    return [join([tensor(g, t, 64), tensor(a1, t, 64), a3[t], a2[t]]) for t in range(4)]


def quad_kernel(g, a1, a3, a2, out3, stats, message3, out_far, stats_far, message):
    q, k, v, do = fours(g, a1, a3, a2)
    ((more, total),) = attend((q, k, v))
    old = [join([stats[i, :64], stats[i, ROWS : ROWS + 64]]) for i in range(2)]
    old = stack([old, unflatten(message3[...])])
    stat, kept, added = combine(old, total, dotted(do, more))
    out_far[...] = join([out3[:64] * kept[:64] + more[:64] * added[:64], out3[64:]])
    stats_far[0], stats_far[1] = stat
    message[...] = flatten(stack([rows_of(stat, 64 * z, 64 * z + 32) for z in range(4)]))


def rest_kernel(
    m0, m1, m2, m3, outs, stats, below, g, a1, a3, a2, out_far, stats_three, stats_far, far5,
    message5, c0, c1, c2, c3,
):
    refs = (m0, m1, m2, m3)
    own = [tensor(g, t) for t in range(4)]
    three = [join([tensor(g, t), tensor(a1, t)]) for t in range(4)]
    four = fours(g, a1, a3, a2)
    five = [
        join([four[t][64 * z : 64 * z + 32] for z in range(4)] + [far5[z, t] for z in range(4)])
        for t in range(4)
    ]
    blocks = []
    for rows, gathered in ((128, three), (64, four), (32, five)):
        mine = [part[:rows] for part in own]
        blocks.append((mine[0], gathered[1], gathered[2], mine[3]))
        blocks.append((gathered[0], mine[1], mine[2], gathered[3]))
    for pair in (0, 2):
        k, v = (join([tensor(refs[pair], t), tensor(refs[pair + 1], t)]) for t in (1, 2))
        q, do = (join([tensor(refs[pair], t, 32), tensor(refs[pair + 1], t, 32)]) for t in (0, 3))
        blocks.append((q, k, v, do))
    k, v = (join([tensor(ref, t, 64) for ref in refs]) for t in (1, 2))
    q, do = (join([tensor(ref, t, 32) for ref in refs]) for t in (0, 3))
    blocks.append((q, k, v, do))
    ((more, total),) = attend(five[:3])
    scores, grads = products(blocks)
    four_stat = [stats_far[0], stats_far[1]]
    three_stat = [stats_three[0], stats_three[1]]
    old = stack(
        [rows_of(four_stat, 64 * z, 64 * z + 32) for z in range(4)] + [unflatten(message5[...])]
    )
    stat5, kept, added = combine(old, total, dotted(five[3], more))
    stat4 = stack(
        [
            rows
            for z in range(4)
            for rows in (
                rows_of(stat5, 32 * z, 32 * z + 32),
                rows_of(four_stat, 64 * z + 32, 64 * z + 64),
            )
        ]
    )
    stat3 = stack(
        [
            rows
            for z in range(2)
            for rows in (
                rows_of(stat4, 64 * z, 64 * z + 64),
                rows_of(three_stat, ROWS * z + 64, ROWS * z + ROWS),
            )
        ]
    )
    own_stat = rows_of(stat3, 0, ROWS)
    out = join([out_far[:32] * kept[:32] + more[:32] * added[:32], out_far[32:]])
    near = group([stats[chip, 0] for chip in range(4)])
    out = out + group([outs[chip] for chip in range(4)]) * jnp.exp(near - own_stat[0])
    stat = [[ungroup(own_stat[i], chip) for i in range(2)] for chip in range(4)]
    block_stats = []
    for rows, gathered in ((128, stat3), (64, stat4), (32, stat5)):
        block_stats += [rows_of(own_stat, 0, rows), gathered]
    block_stats += [stack(stat[:2]), stack(stat[2:]), stack(stat)]
    found = scored(scores, grads, block_stats)
    dqs = [nn(found[i][1], blocks[i][1]) for i in (0, 2, 4, 6, 7, 8)]
    dks = [tn(found[i][1], blocks[i][0]) for i in (1, 3, 5, 6, 7, 8)]
    dvs = [tn(found[i][0], blocks[i][3]) for i in (1, 3, 5, 6, 7, 8)]
    dq, dk, dv = (
        join([f[:32] + g[:32] + h, f[32:64] + g[32:], f[64:]]) for f, g, h, *_ in (dqs, dks, dvs)
    )
    sums = [
        [
            dqs[3 + chip // 2][chip % 2 * 32 : chip % 2 * 32 + 32],
            dks[3 + chip // 2][chip % 2 * ROWS : chip % 2 * ROWS + ROWS],
            dvs[3 + chip // 2][chip % 2 * ROWS : chip % 2 * ROWS + ROWS],
        ]
        for chip in range(4)
    ]
    parts = dqs[5], dks[5], dvs[5]
    for chip, message in enumerate((c0, c1, c2, c3)):
        message[:ROWS] = join([ungroup(out, chip), outs[chip, 32:]]).astype(BF16)
        rows = sums[chip][0] + parts[0][chip * 32 : (chip + 1) * 32] + ungroup(dq, chip)
        message[ROWS : 2 * ROWS] = join([rows, below[chip, 0, 32:]]).astype(BF16)
        for i, top in ((1, dk), (2, dv)):
            whole = below[chip, i] + sums[chip][i]
            part = parts[i][chip * 64 : (chip + 1) * 64]
            rows = join([whole[:32] + part[:32] + ungroup(top, chip), whole[32:64] + part[32:], whole[64:]])
            message[(i + 1) * ROWS : (i + 2) * ROWS] = rows.astype(BF16)
        message[BODY:] = pack(
            [join([stat[chip][i], stats[chip, i, 32:]]) for i in range(2)]
        )


def finish_kernel(steps, q, k, v, do, theirs, places, outs, stats, others, c0, c1, *refs):
    mine_out, theirs_out = refs[-2:]
    messages = (c0, c1)
    tensors = [chip_rows(step, (q, k, v, do), theirs) for step in steps]
    scores, grads = products(tensors)
    terms = [nt(message[BODY:], places[step]) for step, message in zip(steps, messages)]
    finals = [unflatten(rows[:8] + rows[8:16] + rows[16:24]) for rows in terms]
    stat = [[others[step, i] + final[i] for i in range(2)] for step, final in zip(steps, finals)]
    back = [
        nn(places[step], side_by_side([tensor(message, t) for t in range(4)]))
        for step, message in zip(steps, messages)
    ]
    found = scored(scores, grads, stat)
    own = [
        [outs[step] * jnp.exp(stats[step, 0] - stat[slot][0]) for slot, step in enumerate(steps)],
        [nn(score, rows[1]) for (_, score), rows in zip(found, tensors)],
        [tn(score, rows[0]) for (_, score), rows in zip(found, tensors)],
        [tn(chance, rows[3]) for (chance, _), rows in zip(found, tensors)],
    ]
    for slot in range(2):
        for t in range(4):
            rows = own[t][slot] + back[slot][:, t * WIDTH : (t + 1) * WIDTH]
            mine_out[slot, t] = rows[:ROWS].astype(BF16)
            theirs_out[slot, t] = rows[ROWS:].astype(BF16)


def early_kernel(mine0, theirs0, rows):
    for t in range(4):
        for slot in range(2):
            rows[t, :, lanes(own_head(slot))] = mine0[slot, t]
            rows[t, :, lanes(other_head(slot))] = theirs0[slot, t]


def place_kernel(early, mine1, theirs1, att, dq, dk, dv, rows, sems):
    copies = [
        pltpu.make_async_copy(rows.at[t], ref, sems.at[t])
        for t, ref in enumerate((att, dq, dk, dv))
    ]
    for t in range(4):
        rows[t] = early[t]
        for slot in range(2):
            rows[t, :, lanes(own_head(2 + slot))] = mine1[slot, t]
            rows[t, :, lanes(other_head(2 + slot))] = theirs1[slot, t]
        copies[t].start()
    for copy in copies:
        copy.wait()


VMEM = pl.BlockSpec(memory_space=pltpu.VMEM)
LEFT = pl.BlockSpec(memory_space=pltpu.HBM)


def call(kernel, name, outs, *args, left=0, scratch=(), out_specs=None):
    stay = [pltpu.with_memory_space_constraint(arg, pltpu.HBM) for arg in args[:left]]
    args = (*stay, *args[left:])
    return pl.pallas_call(
        kernel,
        name=name,
        out_shape=tuple(jax.ShapeDtypeStruct(shape, dtype) for shape, dtype in outs),
        in_specs=[LEFT] * left + [VMEM] * (len(args) - left),
        out_specs=out_specs or (VMEM,) * len(outs),
        scratch_shapes=scratch,
        compiler_params=pltpu.CompilerParams(vmem_limit_bytes=40 * 2**20),
    )(*args)


def in_plane(array, flip):
    moves = [(PLANE * z + i, PLANE * z + (i ^ flip)) for z in range(DEPTH) for i in range(PLANE)]
    return lax.ppermute(array, "ctx", moves)


def across(array, flip):
    moves = [(PLANE * z + i, PLANE * (z ^ flip) + i) for z in range(DEPTH) for i in range(PLANE)]
    return lax.ppermute(array, "ctx", moves)


def shards(queries, keys, values, out_grad, offsets):
    whole = ((ROWS, HEADS * WIDTH), BF16)
    half = ((CHIPS, 4, ROWS, WIDTH), BF16)
    pairs = ((2, 4, ROWS, WIDTH), BF16)
    message = ((MESSAGE, WIDTH), BF16)
    flat = ((8, WIDTH), F32)
    rows = ((ROWS, WIDTH), F32)
    quads = ((4, ROWS, WIDTH), F32)
    quad_stats = ((4, 2, ROWS, WIDTH), F32)
    chips = ((CHIPS, CHIP, WIDTH), F32)
    chip_stats = ((CHIPS, 2, CHIP, WIDTH), F32)
    seg_stats = ((2, SEG, WIDTH), F32)
    *raw, theirs = call(
        split_kernel, "split", [whole] * 4 + [half], queries, keys, values, out_grad,
        left=4, scratch=[pltpu.SemaphoreType.DMA((4,))],
    )
    theirs = in_plane(theirs, 1)
    picks, places = call(
        maps_kernel, "maps", [((CHIPS, ROWS, CHIP), BF16), ((CHIPS, CHIP, ROWS), BF16)], offsets,
        left=1, scratch=[pltpu.SMEM((6, HEADS), jnp.int32), pltpu.SemaphoreType.DMA((1,))],
    )
    *sent, outs0, stats0 = call(
        chip_kernel, "chip", [message] * 4 + [chips, chip_stats], *raw, theirs, picks
    )
    (others,) = call(alone_kernel, "alone", [chip_stats], places, stats0)
    got = [sent[0]] + [in_plane(sent[step], 2 * step) for step in (1, 2, 3)]
    outs, stats, g, g4 = call(
        near_kernel, "near", [quads, quad_stats, message, ((4, 64, WIDTH), BF16)], *got
    )
    (below,) = call(below_kernel, "below", [((4, 3, ROWS, WIDTH), F32)], *got, stats)
    a1 = across(g, 1)
    a3 = across(g4, 3)
    a2 = across(g4, 2)
    out3, stats3, message3 = call(
        pair_kernel, "pair", [rows, seg_stats, flat], g, a1
    )
    a3, a2, message3 = lax.optimization_barrier((a3, a2, across(message3, 3)))
    fars = (g, a1, a3, a2)
    (top,) = call(top_kernel, "top", [((4, 4, 32, WIDTH), BF16)], *fars)
    top = across(top, 6)
    out_far, stats_far, message5 = call(
        quad_kernel, "quad", [rows, seg_stats, flat], *fars, out3, stats3, message3
    )
    message5 = across(message5, 6)
    back = call(
        rest_kernel, "rest", [message] * 4,
        *got, outs, stats, below, *fars, out_far, stats3, stats_far, top, message5,
    )
    back = [back[0]] + [in_plane(back[step], 2 * step) for step in (1, 2, 3)]
    halves, after = [], ()
    for steps in ((0, 1), (2, 3)):
        mine, other = call(
            functools.partial(finish_kernel, steps), "finish", [pairs, pairs],
            *raw, theirs, places, outs0, stats0, others, *(back[step] for step in steps), *after,
        )
        after = (mine,)
        halves.append((mine, in_plane(other, 1)))
    (mine0, theirs0), (mine1, theirs1) = halves
    (early,) = call(early_kernel, "early", [((4, ROWS, HEADS * WIDTH), BF16)], mine0, theirs0)
    return call(
        place_kernel, "place", [whole] * 4, early, mine1, theirs1, out_specs=(LEFT,) * 4,
        scratch=[pltpu.VMEM((4, ROWS, HEADS * WIDTH), BF16), pltpu.SemaphoreType.DMA((4,))],
    )


def solution(mesh):
    rows = P(("dp", "ctx"), None)
    return jax.shard_map(
        shards,
        mesh=mesh,
        in_specs=(rows,) * 4 + (P("dp", None),),
        out_specs=(rows,) * 4,
        check_vma=False,
    )
```

```python
import functools
import math

import jax
import jax.numpy as jnp
from jax import lax
from jax.experimental import pallas as pl
from jax.experimental.pallas import tpu as pltpu
from jax.sharding import PartitionSpec as P

HEADS = 8
WIDTH = 128
ROWS = 128
CHIP = 2 * ROWS
CHIPS = 4
PLANE = 2 * CHIPS
DEPTH = 8
SEG = 256
BODY = 4 * ROWS
MESSAGE = BODY + 32
SCALE = 1.0 / math.sqrt(WIDTH)
F32 = jnp.float32
BF16 = jnp.bfloat16


def nt(a, b):
    return lax.dot_general(a, b, (((1,), (1,)), ((), ())), preferred_element_type=F32)


def nn(a, b):
    return lax.dot_general(a, b, (((1,), (0,)), ((), ())), preferred_element_type=F32)


def tn(a, b):
    return lax.dot_general(a, b, (((0,), (0,)), ((), ())), preferred_element_type=F32)


def join(parts):
    return jnp.concatenate(parts, axis=0)


def attend(*blocks):
    scores = [nt(q, k) * SCALE for q, k, _ in blocks]
    peaks = [jnp.max(s, axis=1, keepdims=True) for s in scores]
    grown = [jnp.exp(s - peak) for s, peak in zip(scores, peaks)]
    masses = [jnp.sum(g, axis=1, keepdims=True) for g in grown]
    weights = [(g * (1.0 / mass)).astype(BF16) for g, mass in zip(grown, masses)]
    outs = [nn(w, v) for w, (_, _, v) in zip(weights, blocks)]
    return [(o, wide(peak + jnp.log(mass))) for o, peak, mass in zip(outs, peaks, masses)]


def dotted(a, b):
    return wide(jnp.sum(a.astype(F32) * b, axis=1, keepdims=True))


def wide(column):
    return jnp.broadcast_to(column, (column.shape[0], WIDTH))


def across_lanes(column):
    return jnp.concatenate([column, column], axis=1)


def rows_of(stat, begin, end):
    return [column[begin:end] for column in stat]


def stack(stats):
    return [join([stat[i] for stat in stats]) for i in range(2)]


def combine(stat, total, delta):
    peak = jnp.maximum(stat[0], total)
    kept, added = jnp.exp(stat[0] - peak), jnp.exp(total - peak)
    mass = kept + added
    share = 1.0 / mass
    kept, added = kept * share, added * share
    return [peak + jnp.log(mass), kept * stat[1] + added * delta], kept, added


def flatten(stat):
    lane = lax.broadcasted_iota(jnp.int32, (1, WIDTH), 1)
    return jnp.where(lane & 4 == 0, stat[0], stat[1]).T[:8]


def unflatten(flat):
    return [jnp.broadcast_to(flat[i : i + 1], (WIDTH, flat.shape[1])).T for i in (0, 4)]


def three_terms(values):
    high = values.astype(BF16).astype(F32)
    middle = (values - high).astype(BF16).astype(F32)
    return [term.astype(BF16) for term in (high, middle, values - high - middle)]


def pack(stat):
    flat = flatten(stat)
    return join([term.astype(F32) for term in three_terms(flat)] + [jnp.zeros_like(flat)]).astype(BF16)


def unpack(rows):
    terms = rows.astype(F32)
    return unflatten(terms[:8] + terms[8:16] + terms[16:24])


def products(blocks):
    return [nt(q, k) for q, k, _, _ in blocks], [nt(do, v) for _, _, v, do in blocks]


def fit(column, columns):
    return across_lanes(column) if columns == SEG else column[:, :columns]


def scored(scores, grads, stats):
    chances = [
        jnp.exp(s * SCALE - fit(stat[0], s.shape[1])) for s, stat in zip(scores, stats)
    ]
    parts = [
        (chance * (grad - fit(stat[1], grad.shape[1])) * SCALE).astype(BF16)
        for chance, grad, stat in zip(chances, grads, stats)
    ]
    return [(chance.astype(BF16), part) for chance, part in zip(chances, parts)]


def position(offs, head, i):
    place = (offs[2, head] ^ 2) + 4 * (i - 64)
    for below, level, flip, begin in ((64, 3, 4, 32), (32, 4, 8, 16), (16, 5, 16, 8), (8, 5, 0, 0)):
        stride = 32 if level == 5 else 2**level
        place = jnp.where(i < below, (offs[level, head] ^ flip) + stride * (i - begin), place)
    return place


def picking(offs, head):
    i = lax.broadcasted_iota(jnp.int32, (ROWS, WIDTH), 0)
    lane = lax.broadcasted_iota(jnp.int32, (ROWS, WIDTH), 1)
    place = position(offs, head, i)
    hits = [jnp.where(place == lane + begin, 1.0, 0.0).astype(BF16) for begin in (0, WIDTH)]
    return jnp.concatenate(hits, axis=1)


def placing(offs, head):
    place = position(offs, head, lax.broadcasted_iota(jnp.int32, (1, WIDTH), 1))
    row = lax.broadcasted_iota(jnp.int32, (CHIP, WIDTH), 0)
    return jnp.where(row == place, 1.0, 0.0).astype(BF16)


def side_by_side(parts):
    return jnp.concatenate(parts, axis=1)


def lanes(head):
    return pl.ds(pl.multiple_of(head * WIDTH, WIDTH), WIDTH)


def own_head(step):
    spot = lax.axis_index("ctx") % PLANE
    return spot ^ (2 * step)


def other_head(step):
    return own_head(step) ^ 1


def split_kernel(q, k, v, do, q_in, k_in, v_in, do_in, theirs, sems):
    inside = (q_in, k_in, v_in, do_in)
    copies = [
        pltpu.make_async_copy(ref, to, sems.at[t])
        for t, (ref, to) in enumerate(zip((q, k, v, do), inside))
    ]
    for copy in copies:
        copy.start()
    for t, ref in enumerate(inside):
        copies[t].wait()
        for step in range(CHIPS):
            theirs[step, t] = ref[:, lanes(other_head(step))]


def chip_rows(step, raw, theirs):
    head = own_head(step)
    return [join([ref[:, lanes(head)], theirs[step, t]]) for t, ref in enumerate(raw)]


def maps_kernel(offs_left, picks, places, offs, sem):
    copy = pltpu.make_async_copy(offs_left, offs, sem.at[0])
    copy.start()
    copy.wait()
    for step in range(CHIPS):
        picks[step] = picking(offs, own_head(step))
        places[step] = placing(offs, own_head(step))


def chip_kernel(steps, q, k, v, do, theirs, picks, *refs):
    messages, (outs, stats) = refs[:-2], refs[-2:]
    tensors = [chip_rows(step, (q, k, v, do), theirs) for step in steps]
    found = attend(*(rows[:3] for rows in tensors))
    picked = [nn(picks[step], side_by_side(rows)) for step, rows in zip(steps, tensors)]
    deltas = [dotted(rows[3], out) for rows, (out, _) in zip(tensors, found)]
    for slot, message in enumerate(messages):
        for t in range(4):
            rows = picked[slot][:, t * WIDTH : (t + 1) * WIDTH]
            message[t * ROWS : (t + 1) * ROWS] = rows.astype(BF16)
    lane = lax.broadcasted_iota(jnp.int32, (1, WIDTH), 1)
    for slot, (step, message) in enumerate(zip(steps, messages)):
        out, total = found[slot]
        outs[slot] = out
        stats[slot, 0] = total
        stats[slot, 1] = deltas[slot]
        flat = jnp.where(lane & 4 == 0, total, deltas[slot]).T[:8]
        flat = nt(join([term.astype(F32) for term in three_terms(flat)]).astype(BF16), picks[step])
        message[BODY:] = join([flat, jnp.zeros((8, WIDTH), F32)]).astype(BF16)


def alone_kernel(places, stats_own, stats_sent, others):
    for step in range(CHIPS):
        alone = 1.0 - nn(places[step], jnp.ones((ROWS, WIDTH), BF16))
        for i in range(2):
            stat = stats_sent[step - 1, i] if step else stats_own[0, i]
            others[step, i] = stat * alone


def tensor(ref, t, rows=ROWS):
    return ref[t * ROWS : t * ROWS + rows]


def group(parts):
    return join(
        [p[:8] for p in parts] + [p[8:16] for p in parts] + [p[16:32] for p in parts]
    )


def ungroup(rows, chip):
    return join(
        [
            rows[8 * chip : 8 * chip + 8],
            rows[32 + 8 * chip : 40 + 8 * chip],
            rows[64 + 16 * chip : 80 + 16 * chip],
        ]
    )


def near_kernel(m0, m1, m2, m3, outs, stats, g, g4):
    refs = (m0, m1, m2, m3)
    stat = [unpack(ref[BODY:]) for ref in refs]
    out = [None] * 4
    blocks = [
        [join([tensor(refs[pair], t), tensor(refs[pair + 1], t)]) for t in range(4)]
        for pair in (0, 2)
    ]
    blocks.append([join([tensor(ref, t, 64) for ref in refs]) for t in range(4)])
    found = attend(*(block[:3] for block in blocks))
    deltas = [dotted(block[3], more) for block, (more, _) in zip(blocks, found)]
    for pair in (0, 2):
        more, total = found[pair // 2]
        joined, _, added = combine(stack(stat[pair : pair + 2]), total, deltas[pair // 2])
        more = more * added
        for chip in range(2):
            out[pair + chip] = more[chip * ROWS : (chip + 1) * ROWS]
            stat[pair + chip] = rows_of(joined, chip * ROWS, (chip + 1) * ROWS)
    more, total = found[2]
    joined, kept, added = combine(stack([rows_of(s, 0, 64) for s in stat]), total, deltas[2])
    more = join([o[:64] for o in out]) * kept + more * added
    for chip in range(4):
        out[chip] = join([more[chip * 64 : (chip + 1) * 64], out[chip][64:]])
        stat[chip] = stack(
            [rows_of(joined, chip * 64, (chip + 1) * 64), rows_of(stat[chip], 64, ROWS)]
        )
        outs[chip] = out[chip]
        stats[chip, 0], stats[chip, 1] = stat[chip]
    for t in range(4):
        rows = group([tensor(ref, t, 32).astype(F32) for ref in refs])
        rows = rows.astype(BF16)
        g[t * ROWS : (t + 1) * ROWS] = rows
        g4[t] = rows[:64]
    g[BODY:] = pack([group([s[i] for s in stat]) for i in range(2)])


def below_kernel(m0, m1, m2, m3, stats, sums):
    refs = (m0, m1, m2, m3)
    stat = [[stats[chip, i] for i in range(2)] for chip in range(4)]
    tensors = [[tensor(ref, t) for t in range(4)] for ref in refs]
    blocks, block_stats = [], []
    for pair in (0, 2):
        k, v = (join([tensors[pair][t], tensors[pair + 1][t]]) for t in (1, 2))
        q, do = (join([tensors[pair][t][32:], tensors[pair + 1][t][32:]]) for t in (0, 3))
        blocks.append((q, k, v, do))
        block_stats.append(stack([rows_of(s, 32, ROWS) for s in stat[pair : pair + 2]]))
    k, v = (join([rows[t][:64] for rows in tensors]) for t in (1, 2))
    q, do = (join([rows[t][32:64] for rows in tensors]) for t in (0, 3))
    blocks.append((q, k, v, do))
    block_stats.append(stack([rows_of(s, 32, 64) for s in stat]))
    found = scored(*products(blocks), block_stats)
    dqs = [nn(score, block[1]) for (_, score), block in zip(found, blocks)]
    dks = [tn(score, block[0]) for (_, score), block in zip(found, blocks)]
    dvs = [tn(chance, block[3]) for (chance, _), block in zip(found, blocks)]
    whole = [
        [
            dqs[chip // 2][chip % 2 * 96 : chip % 2 * 96 + 96],
            dks[chip // 2][chip % 2 * ROWS : chip % 2 * ROWS + ROWS],
            dvs[chip // 2][chip % 2 * ROWS : chip % 2 * ROWS + ROWS],
        ]
        for chip in range(4)
    ]
    parts = dqs[2], dks[2], dvs[2]
    for chip in range(4):
        sums[chip, 0, :32] = jnp.zeros((32, WIDTH), F32)
        sums[chip, 0, 32:64] = whole[chip][0][:32] + parts[0][chip * 32 : (chip + 1) * 32]
        sums[chip, 0, 64:] = whole[chip][0][32:]
        for i in (1, 2):
            sums[chip, i, :64] = whole[chip][i][:64] + parts[i][chip * 64 : (chip + 1) * 64]
            sums[chip, i, 64:] = whole[chip][i][64:]


def pair_kernel(g, a1, out3, stats, message):
    refs = (g, a1)
    q, k, v, do = (join([tensor(ref, t) for ref in refs]) for t in range(4))
    ((more, total),) = attend((q, k, v))
    stat, _, added = combine(stack([unpack(ref[BODY:]) for ref in refs]), total, dotted(do, more))
    out3[...] = more[:ROWS] * added[:ROWS]
    stats[0], stats[1] = stat
    message[...] = flatten(stack([rows_of(stat, 0, 64), rows_of(stat, ROWS, ROWS + 64)]))


def top_kernel(g, a1, a3, a2, top):
    for t in range(4):
        top[0, t] = tensor(g, t, 32)
        top[1, t] = tensor(a1, t, 32)
        top[2, t] = a3[t, :32]
        top[3, t] = a2[t, :32]


def fours(g, a1, a3, a2):
    return [join([tensor(g, t, 64), tensor(a1, t, 64), a3[t], a2[t]]) for t in range(4)]


def quad_kernel(g, a1, a3, a2, out3, stats, message3, out_far, stats_far, message):
    q, k, v, do = fours(g, a1, a3, a2)
    ((more, total),) = attend((q, k, v))
    old = [join([stats[i, :64], stats[i, ROWS : ROWS + 64]]) for i in range(2)]
    old = stack([old, unflatten(message3[...])])
    stat, kept, added = combine(old, total, dotted(do, more))
    out_far[...] = join([out3[:64] * kept[:64] + more[:64] * added[:64], out3[64:]])
    stats_far[0], stats_far[1] = stat
    message[...] = flatten(stack([rows_of(stat, 64 * z, 64 * z + 32) for z in range(4)]))


def rest_kernel(
    m0, m1, m2, m3, outs, stats, below, g, a1, a3, a2, out_far, stats_three, stats_far, far5,
    message5, c0, c1, c2, c3,
):
    refs = (m0, m1, m2, m3)
    own = [tensor(g, t) for t in range(4)]
    three = [join([tensor(g, t), tensor(a1, t)]) for t in range(4)]
    four = fours(g, a1, a3, a2)
    five = [
        join([four[t][64 * z : 64 * z + 32] for z in range(4)] + [far5[z, t] for z in range(4)])
        for t in range(4)
    ]
    blocks = []
    for rows, gathered in ((128, three), (64, four), (32, five)):
        mine = [part[:rows] for part in own]
        blocks.append((mine[0], gathered[1], gathered[2], mine[3]))
        blocks.append((gathered[0], mine[1], mine[2], gathered[3]))
    for pair in (0, 2):
        k, v = (join([tensor(refs[pair], t), tensor(refs[pair + 1], t)]) for t in (1, 2))
        q, do = (join([tensor(refs[pair], t, 32), tensor(refs[pair + 1], t, 32)]) for t in (0, 3))
        blocks.append((q, k, v, do))
    k, v = (join([tensor(ref, t, 64) for ref in refs]) for t in (1, 2))
    q, do = (join([tensor(ref, t, 32) for ref in refs]) for t in (0, 3))
    blocks.append((q, k, v, do))
    ((more, total),) = attend(five[:3])
    scores, grads = products(blocks)
    four_stat = [stats_far[0], stats_far[1]]
    three_stat = [stats_three[0], stats_three[1]]
    old = stack(
        [rows_of(four_stat, 64 * z, 64 * z + 32) for z in range(4)] + [unflatten(message5[...])]
    )
    stat5, kept, added = combine(old, total, dotted(five[3], more))
    stat4 = stack(
        [
            rows
            for z in range(4)
            for rows in (
                rows_of(stat5, 32 * z, 32 * z + 32),
                rows_of(four_stat, 64 * z + 32, 64 * z + 64),
            )
        ]
    )
    stat3 = stack(
        [
            rows
            for z in range(2)
            for rows in (
                rows_of(stat4, 64 * z, 64 * z + 64),
                rows_of(three_stat, ROWS * z + 64, ROWS * z + ROWS),
            )
        ]
    )
    own_stat = rows_of(stat3, 0, ROWS)
    out = join([out_far[:32] * kept[:32] + more[:32] * added[:32], out_far[32:]])
    near = group([stats[chip, 0] for chip in range(4)])
    out = out + group([outs[chip] for chip in range(4)]) * jnp.exp(near - own_stat[0])
    stat = [[ungroup(own_stat[i], chip) for i in range(2)] for chip in range(4)]
    block_stats = []
    for rows, gathered in ((128, stat3), (64, stat4), (32, stat5)):
        block_stats += [rows_of(own_stat, 0, rows), gathered]
    block_stats += [stack(stat[:2]), stack(stat[2:]), stack(stat)]
    found = scored(scores, grads, block_stats)
    dqs = [nn(found[i][1], blocks[i][1]) for i in (0, 2, 4, 6, 7, 8)]
    dks = [tn(found[i][1], blocks[i][0]) for i in (1, 3, 5, 6, 7, 8)]
    dvs = [tn(found[i][0], blocks[i][3]) for i in (1, 3, 5, 6, 7, 8)]
    dq, dk, dv = (
        join([f[:32] + g[:32] + h, f[32:64] + g[32:], f[64:]]) for f, g, h, *_ in (dqs, dks, dvs)
    )
    sums = [
        [
            dqs[3 + chip // 2][chip % 2 * 32 : chip % 2 * 32 + 32],
            dks[3 + chip // 2][chip % 2 * ROWS : chip % 2 * ROWS + ROWS],
            dvs[3 + chip // 2][chip % 2 * ROWS : chip % 2 * ROWS + ROWS],
        ]
        for chip in range(4)
    ]
    parts = dqs[5], dks[5], dvs[5]
    for chip, message in enumerate((c0, c1, c2, c3)):
        message[:ROWS] = join([ungroup(out, chip), outs[chip, 32:]]).astype(BF16)
        rows = sums[chip][0] + parts[0][chip * 32 : (chip + 1) * 32] + ungroup(dq, chip)
        message[ROWS : 2 * ROWS] = join([rows, below[chip, 0, 32:]]).astype(BF16)
        for i, top in ((1, dk), (2, dv)):
            whole = below[chip, i] + sums[chip][i]
            part = parts[i][chip * 64 : (chip + 1) * 64]
            rows = join([whole[:32] + part[:32] + ungroup(top, chip), whole[32:64] + part[32:], whole[64:]])
            message[(i + 1) * ROWS : (i + 2) * ROWS] = rows.astype(BF16)
        message[BODY:] = pack(
            [join([stat[chip][i], stats[chip, i, 32:]]) for i in range(2)]
        )


def finish_kernel(steps, q, k, v, do, theirs, places, outs_own, outs_sent, stats_own,
    stats_sent, others, c0, c1, *refs):
    mine_out, theirs_out = refs[-2:]
    messages = (c0, c1)
    tensors = [chip_rows(step, (q, k, v, do), theirs) for step in steps]
    scores, grads = products(tensors)
    terms = [nt(message[BODY:], places[step]) for step, message in zip(steps, messages)]
    finals = [unflatten(rows[:8] + rows[8:16] + rows[16:24]) for rows in terms]
    stat = [[others[step, i] + final[i] for i in range(2)] for step, final in zip(steps, finals)]
    back = [
        nn(places[step], side_by_side([tensor(message, t) for t in range(4)]))
        for step, message in zip(steps, messages)
    ]
    found = scored(scores, grads, stat)
    own = [
        [
            (outs_sent[step - 1] if step else outs_own[0])
            * jnp.exp((stats_sent[step - 1, 0] if step else stats_own[0, 0]) - stat[slot][0])
            for slot, step in enumerate(steps)
        ],
        [nn(score, rows[1]) for (_, score), rows in zip(found, tensors)],
        [tn(score, rows[0]) for (_, score), rows in zip(found, tensors)],
        [tn(chance, rows[3]) for (chance, _), rows in zip(found, tensors)],
    ]
    for slot in range(2):
        for t in range(4):
            rows = own[t][slot] + back[slot][:, t * WIDTH : (t + 1) * WIDTH]
            mine_out[slot, t] = rows[:ROWS].astype(BF16)
            theirs_out[slot, t] = rows[ROWS:].astype(BF16)


def early_kernel(mine0, theirs0, rows):
    for t in range(4):
        for slot in range(2):
            rows[t, :, lanes(own_head(slot))] = mine0[slot, t]
            rows[t, :, lanes(other_head(slot))] = theirs0[slot, t]


def place_kernel(early, mine1, theirs1, att, dq, dk, dv, rows, sems):
    copies = [
        pltpu.make_async_copy(rows.at[t], ref, sems.at[t])
        for t, ref in enumerate((att, dq, dk, dv))
    ]
    for t in range(4):
        rows[t] = early[t]
        for slot in range(2):
            rows[t, :, lanes(own_head(2 + slot))] = mine1[slot, t]
            rows[t, :, lanes(other_head(2 + slot))] = theirs1[slot, t]
        copies[t].start()
    for copy in copies:
        copy.wait()


VMEM = pl.BlockSpec(memory_space=pltpu.VMEM)
LEFT = pl.BlockSpec(memory_space=pltpu.HBM)


def call(kernel, name, outs, *args, left=0, scratch=(), out_specs=None):
    stay = [pltpu.with_memory_space_constraint(arg, pltpu.HBM) for arg in args[:left]]
    args = (*stay, *args[left:])
    return pl.pallas_call(
        kernel,
        name=name,
        out_shape=tuple(jax.ShapeDtypeStruct(shape, dtype) for shape, dtype in outs),
        in_specs=[LEFT] * left + [VMEM] * (len(args) - left),
        out_specs=out_specs or (VMEM,) * len(outs),
        scratch_shapes=scratch,
        compiler_params=pltpu.CompilerParams(vmem_limit_bytes=40 * 2**20),
    )(*args)


def in_plane(array, flip):
    moves = [(PLANE * z + i, PLANE * z + (i ^ flip)) for z in range(DEPTH) for i in range(PLANE)]
    return lax.ppermute(array, "ctx", moves)


def across(array, flip):
    moves = [(PLANE * z + i, PLANE * (z ^ flip) + i) for z in range(DEPTH) for i in range(PLANE)]
    return lax.ppermute(array, "ctx", moves)


def shards(queries, keys, values, out_grad, offsets):
    whole = ((ROWS, HEADS * WIDTH), BF16)
    half = ((CHIPS, 4, ROWS, WIDTH), BF16)
    pairs = ((2, 4, ROWS, WIDTH), BF16)
    message = ((MESSAGE, WIDTH), BF16)
    flat = ((8, WIDTH), F32)
    rows = ((ROWS, WIDTH), F32)
    quads = ((4, ROWS, WIDTH), F32)
    quad_stats = ((4, 2, ROWS, WIDTH), F32)
    chips = ((CHIPS, CHIP, WIDTH), F32)
    chip_stats = ((CHIPS, 2, CHIP, WIDTH), F32)
    seg_stats = ((2, SEG, WIDTH), F32)
    *raw, theirs = call(
        split_kernel, "split", [whole] * 4 + [half], queries, keys, values, out_grad,
        left=4, scratch=[pltpu.SemaphoreType.DMA((4,))],
    )
    theirs = in_plane(theirs, 1)
    picks, places = call(
        maps_kernel, "maps", [((CHIPS, ROWS, CHIP), BF16), ((CHIPS, CHIP, ROWS), BF16)], offsets,
        left=1, scratch=[pltpu.SMEM((6, HEADS), jnp.int32), pltpu.SemaphoreType.DMA((1,))],
    )
    found = []
    for steps in ((1, 2, 3), (0,)):
        sizes = [((len(steps), CHIP, WIDTH), F32), ((len(steps), 2, CHIP, WIDTH), F32)]
        found.append(
            call(
                functools.partial(chip_kernel, steps), "chip", [message] * len(steps) + sizes,
                *raw, theirs, picks,
            )
        )
    (*sent, outs_sent, stats_sent), (kept, outs_own, stats_own) = found
    sent = [kept, *sent]
    (others,) = call(alone_kernel, "alone", [chip_stats], places, stats_own, stats_sent)
    got = [sent[0]] + [in_plane(sent[step], 2 * step) for step in (1, 2, 3)]
    outs, stats, g, g4 = call(
        near_kernel, "near", [quads, quad_stats, message, ((4, 64, WIDTH), BF16)], *got
    )
    (below,) = call(below_kernel, "below", [((4, 3, ROWS, WIDTH), F32)], *got, stats)
    a1 = across(g, 1)
    a3 = across(g4, 3)
    a2 = across(g4, 2)
    out3, stats3, message3 = call(
        pair_kernel, "pair", [rows, seg_stats, flat], g, a1
    )
    a3, a2, message3 = lax.optimization_barrier((a3, a2, across(message3, 3)))
    fars = (g, a1, a3, a2)
    (top,) = call(top_kernel, "top", [((4, 4, 32, WIDTH), BF16)], *fars)
    top = across(top, 6)
    out_far, stats_far, message5 = call(
        quad_kernel, "quad", [rows, seg_stats, flat], *fars, out3, stats3, message3
    )
    message5 = across(message5, 6)
    back = call(
        rest_kernel, "rest", [message] * 4,
        *got, outs, stats, below, *fars, out_far, stats3, stats_far, top, message5,
    )
    back = [back[0]] + [in_plane(back[step], 2 * step) for step in (1, 2, 3)]
    halves, after = [], ()
    for steps in ((0, 1), (2, 3)):
        mine, other = call(
            functools.partial(finish_kernel, steps), "finish", [pairs, pairs],
            *raw, theirs, places, outs_own, outs_sent, stats_own, stats_sent, others, *(back[step] for step in steps), *after,
        )
        after = (mine,)
        halves.append((mine, in_plane(other, 1)))
    (mine0, theirs0), (mine1, theirs1) = halves
    (early,) = call(early_kernel, "early", [((4, ROWS, HEADS * WIDTH), BF16)], mine0, theirs0)
    return call(
        place_kernel, "place", [whole] * 4, early, mine1, theirs1, out_specs=(LEFT,) * 4,
        scratch=[pltpu.VMEM((4, ROWS, HEADS * WIDTH), BF16), pltpu.SemaphoreType.DMA((4,))],
    )


def solution(mesh):
    rows = P(("dp", "ctx"), None)
    return jax.shard_map(
        shards,
        mesh=mesh,
        in_specs=(rows,) * 4 + (P("dp", None),),
        out_specs=(rows,) * 4,
        check_vma=False,
    )
```

```python
import functools
import math

import jax
import jax.numpy as jnp
from jax import lax
from jax.experimental import pallas as pl
from jax.experimental.pallas import tpu as pltpu
from jax.sharding import PartitionSpec as P

HEADS = 8
WIDTH = 128
ROWS = 128
CHIP = 2 * ROWS
CHIPS = 4
PLANE = 2 * CHIPS
DEPTH = 8
SEG = 256
BODY = 4 * ROWS
MESSAGE = BODY + 32
SCALE = 1.0 / math.sqrt(WIDTH)
F32 = jnp.float32
BF16 = jnp.bfloat16


def nt(a, b):
    return lax.dot_general(a, b, (((1,), (1,)), ((), ())), preferred_element_type=F32)


def nn(a, b):
    return lax.dot_general(a, b, (((1,), (0,)), ((), ())), preferred_element_type=F32)


def tn(a, b):
    return lax.dot_general(a, b, (((0,), (0,)), ((), ())), preferred_element_type=F32)


def join(parts):
    return jnp.concatenate(parts, axis=0)


def attend(*blocks):
    scores = [nt(q, k) * SCALE for q, k, _ in blocks]
    peaks = [jnp.max(s, axis=1, keepdims=True) for s in scores]
    grown = [jnp.exp(s - peak) for s, peak in zip(scores, peaks)]
    masses = [jnp.sum(g, axis=1, keepdims=True) for g in grown]
    weights = [(g * (1.0 / mass)).astype(BF16) for g, mass in zip(grown, masses)]
    outs = [nn(w, v) for w, (_, _, v) in zip(weights, blocks)]
    return [(o, wide(peak + jnp.log(mass))) for o, peak, mass in zip(outs, peaks, masses)]


def dotted(a, b):
    return wide(jnp.sum(a.astype(F32) * b, axis=1, keepdims=True))


def wide(column):
    return jnp.broadcast_to(column, (column.shape[0], WIDTH))


def across_lanes(column):
    return jnp.concatenate([column, column], axis=1)


def rows_of(stat, begin, end):
    return [column[begin:end] for column in stat]


def stack(stats):
    return [join([stat[i] for stat in stats]) for i in range(2)]


def combine(stat, total, delta):
    peak = jnp.maximum(stat[0], total)
    kept, added = jnp.exp(stat[0] - peak), jnp.exp(total - peak)
    mass = kept + added
    share = 1.0 / mass
    kept, added = kept * share, added * share
    return [peak + jnp.log(mass), kept * stat[1] + added * delta], kept, added


def flatten(stat):
    lane = lax.broadcasted_iota(jnp.int32, (1, WIDTH), 1)
    return jnp.where(lane & 4 == 0, stat[0], stat[1]).T[:8]


def unflatten(flat):
    return [jnp.broadcast_to(flat[i : i + 1], (WIDTH, flat.shape[1])).T for i in (0, 4)]


def three_terms(values):
    high = values.astype(BF16).astype(F32)
    middle = (values - high).astype(BF16).astype(F32)
    return [term.astype(BF16) for term in (high, middle, values - high - middle)]


def pack(stat):
    flat = flatten(stat)
    return join([term.astype(F32) for term in three_terms(flat)] + [jnp.zeros_like(flat)]).astype(BF16)


def unpack(rows):
    terms = rows.astype(F32)
    return unflatten(terms[:8] + terms[8:16] + terms[16:24])


def products(blocks):
    return [nt(q, k) for q, k, _, _ in blocks], [nt(do, v) for _, _, v, do in blocks]


def fit(column, columns):
    return across_lanes(column) if columns == SEG else column[:, :columns]


def scored(scores, grads, stats):
    chances = [
        jnp.exp(s * SCALE - fit(stat[0], s.shape[1])) for s, stat in zip(scores, stats)
    ]
    parts = [
        (chance * (grad - fit(stat[1], grad.shape[1])) * SCALE).astype(BF16)
        for chance, grad, stat in zip(chances, grads, stats)
    ]
    return [(chance.astype(BF16), part) for chance, part in zip(chances, parts)]


def position(offs, head, i):
    place = (offs[2, head] ^ 2) + 4 * (i - 64)
    for below, level, flip, begin in ((64, 3, 4, 32), (32, 4, 8, 16), (16, 5, 16, 8), (8, 5, 0, 0)):
        stride = 32 if level == 5 else 2**level
        place = jnp.where(i < below, (offs[level, head] ^ flip) + stride * (i - begin), place)
    return place


def picking(offs, head):
    i = lax.broadcasted_iota(jnp.int32, (ROWS, WIDTH), 0)
    lane = lax.broadcasted_iota(jnp.int32, (ROWS, WIDTH), 1)
    place = position(offs, head, i)
    hits = [jnp.where(place == lane + begin, 1.0, 0.0).astype(BF16) for begin in (0, WIDTH)]
    return jnp.concatenate(hits, axis=1)


def placing(offs, head):
    place = position(offs, head, lax.broadcasted_iota(jnp.int32, (1, WIDTH), 1))
    row = lax.broadcasted_iota(jnp.int32, (CHIP, WIDTH), 0)
    return jnp.where(row == place, 1.0, 0.0).astype(BF16)


def side_by_side(parts):
    return jnp.concatenate(parts, axis=1)


def lanes(head):
    return pl.ds(pl.multiple_of(head * WIDTH, WIDTH), WIDTH)


def own_head(step):
    spot = lax.axis_index("ctx") % PLANE
    return spot ^ (2 * step)


def other_head(step):
    return own_head(step) ^ 1


def split_kernel(q, k, v, do, q_in, k_in, v_in, do_in, theirs, sems):
    inside = (q_in, k_in, v_in, do_in)
    copies = [
        pltpu.make_async_copy(ref, to, sems.at[t])
        for t, (ref, to) in enumerate(zip((q, k, v, do), inside))
    ]
    for copy in copies:
        copy.start()
    for t, ref in enumerate(inside):
        copies[t].wait()
        for step in range(CHIPS):
            theirs[step, t] = ref[:, lanes(other_head(step))]


def chip_rows(step, raw, theirs):
    head = own_head(step)
    return [join([ref[:, lanes(head)], theirs[step, t]]) for t, ref in enumerate(raw)]


def maps_kernel(offs_left, picks, places, offs, sem):
    copy = pltpu.make_async_copy(offs_left, offs, sem.at[0])
    copy.start()
    copy.wait()
    for step in range(CHIPS):
        picks[step] = picking(offs, own_head(step))
        places[step] = placing(offs, own_head(step))


def chip_kernel(steps, q, k, v, do, theirs, picks, *refs):
    messages, (outs, stats) = refs[:-2], refs[-2:]
    tensors = [chip_rows(step, (q, k, v, do), theirs) for step in steps]
    found = attend(*(rows[:3] for rows in tensors))
    picked = [nn(picks[step], side_by_side(rows)) for step, rows in zip(steps, tensors)]
    deltas = [dotted(rows[3], out) for rows, (out, _) in zip(tensors, found)]
    for slot, message in enumerate(messages):
        for t in range(4):
            rows = picked[slot][:, t * WIDTH : (t + 1) * WIDTH]
            message[t * ROWS : (t + 1) * ROWS] = rows.astype(BF16)
    lane = lax.broadcasted_iota(jnp.int32, (1, WIDTH), 1)
    for slot, (step, message) in enumerate(zip(steps, messages)):
        out, total = found[slot]
        outs[slot] = out
        stats[slot, 0] = total
        stats[slot, 1] = deltas[slot]
        flat = jnp.where(lane & 4 == 0, total, deltas[slot]).T[:8]
        flat = nt(join([term.astype(F32) for term in three_terms(flat)]).astype(BF16), picks[step])
        message[BODY:] = join([flat, jnp.zeros((8, WIDTH), F32)]).astype(BF16)


def alone_kernel(places, stats_own, stats_sent, others):
    for step in range(CHIPS):
        alone = 1.0 - nn(places[step], jnp.ones((ROWS, WIDTH), BF16))
        for i in range(2):
            stat = stats_sent[step - 1, i] if step else stats_own[0, i]
            others[step, i] = stat * alone


def tensor(ref, t, rows=ROWS):
    return ref[t * ROWS : t * ROWS + rows]


def group(parts):
    return join(
        [p[:8] for p in parts] + [p[8:16] for p in parts] + [p[16:32] for p in parts]
    )


def ungroup(rows, chip):
    return join(
        [
            rows[8 * chip : 8 * chip + 8],
            rows[32 + 8 * chip : 40 + 8 * chip],
            rows[64 + 16 * chip : 80 + 16 * chip],
        ]
    )


def first_kernel(m0, m1, first, first_found):
    q, k, v, do = (join([tensor(m0, t), tensor(m1, t)]) for t in range(4))
    ((more, total),) = attend((q, k, v))
    first[...] = more
    first_found[0], first_found[1] = total, dotted(do, more)


def near_kernel(m0, m1, m2, m3, first, first_found, outs, stats, g, g4):
    refs = (m0, m1, m2, m3)
    stat = [unpack(ref[BODY:]) for ref in refs]
    out = [None] * 4
    blocks = [
        [join([tensor(m2, t), tensor(m3, t)]) for t in range(4)],
        [join([tensor(ref, t, 64) for ref in refs]) for t in range(4)],
    ]
    found = attend(*(block[:3] for block in blocks))
    deltas = [dotted(block[3], more) for block, (more, _) in zip(blocks, found)]
    found = [(first[...], first_found[0]), *found]
    deltas = [first_found[1], *deltas]
    for pair in (0, 2):
        more, total = found[pair // 2]
        joined, _, added = combine(stack(stat[pair : pair + 2]), total, deltas[pair // 2])
        more = more * added
        for chip in range(2):
            out[pair + chip] = more[chip * ROWS : (chip + 1) * ROWS]
            stat[pair + chip] = rows_of(joined, chip * ROWS, (chip + 1) * ROWS)
    more, total = found[2]
    joined, kept, added = combine(stack([rows_of(s, 0, 64) for s in stat]), total, deltas[2])
    more = join([o[:64] for o in out]) * kept + more * added
    for chip in range(4):
        out[chip] = join([more[chip * 64 : (chip + 1) * 64], out[chip][64:]])
        stat[chip] = stack(
            [rows_of(joined, chip * 64, (chip + 1) * 64), rows_of(stat[chip], 64, ROWS)]
        )
        outs[chip] = out[chip]
        stats[chip, 0], stats[chip, 1] = stat[chip]
    for t in range(4):
        rows = group([tensor(ref, t, 32).astype(F32) for ref in refs])
        rows = rows.astype(BF16)
        g[t * ROWS : (t + 1) * ROWS] = rows
        g4[t] = rows[:64]
    g[BODY:] = pack([group([s[i] for s in stat]) for i in range(2)])


def below_kernel(m0, m1, m2, m3, stats, sums):
    refs = (m0, m1, m2, m3)
    stat = [[stats[chip, i] for i in range(2)] for chip in range(4)]
    tensors = [[tensor(ref, t) for t in range(4)] for ref in refs]
    blocks, block_stats = [], []
    for pair in (0, 2):
        k, v = (join([tensors[pair][t], tensors[pair + 1][t]]) for t in (1, 2))
        q, do = (join([tensors[pair][t][32:], tensors[pair + 1][t][32:]]) for t in (0, 3))
        blocks.append((q, k, v, do))
        block_stats.append(stack([rows_of(s, 32, ROWS) for s in stat[pair : pair + 2]]))
    k, v = (join([rows[t][:64] for rows in tensors]) for t in (1, 2))
    q, do = (join([rows[t][32:64] for rows in tensors]) for t in (0, 3))
    blocks.append((q, k, v, do))
    block_stats.append(stack([rows_of(s, 32, 64) for s in stat]))
    found = scored(*products(blocks), block_stats)
    dqs = [nn(score, block[1]) for (_, score), block in zip(found, blocks)]
    dks = [tn(score, block[0]) for (_, score), block in zip(found, blocks)]
    dvs = [tn(chance, block[3]) for (chance, _), block in zip(found, blocks)]
    whole = [
        [
            dqs[chip // 2][chip % 2 * 96 : chip % 2 * 96 + 96],
            dks[chip // 2][chip % 2 * ROWS : chip % 2 * ROWS + ROWS],
            dvs[chip // 2][chip % 2 * ROWS : chip % 2 * ROWS + ROWS],
        ]
        for chip in range(4)
    ]
    parts = dqs[2], dks[2], dvs[2]
    for chip in range(4):
        sums[chip, 0, :32] = jnp.zeros((32, WIDTH), F32)
        sums[chip, 0, 32:64] = whole[chip][0][:32] + parts[0][chip * 32 : (chip + 1) * 32]
        sums[chip, 0, 64:] = whole[chip][0][32:]
        for i in (1, 2):
            sums[chip, i, :64] = whole[chip][i][:64] + parts[i][chip * 64 : (chip + 1) * 64]
            sums[chip, i, 64:] = whole[chip][i][64:]


def pair_kernel(g, a1, out3, stats, message):
    refs = (g, a1)
    q, k, v, do = (join([tensor(ref, t) for ref in refs]) for t in range(4))
    ((more, total),) = attend((q, k, v))
    stat, _, added = combine(stack([unpack(ref[BODY:]) for ref in refs]), total, dotted(do, more))
    out3[...] = more[:ROWS] * added[:ROWS]
    stats[0], stats[1] = stat
    message[...] = flatten(stack([rows_of(stat, 0, 64), rows_of(stat, ROWS, ROWS + 64)]))


def top_kernel(g, a1, a3, a2, top):
    for t in range(4):
        top[0, t] = tensor(g, t, 32)
        top[1, t] = tensor(a1, t, 32)
        top[2, t] = a3[t, :32]
        top[3, t] = a2[t, :32]


def fours(g, a1, a3, a2):
    return [join([tensor(g, t, 64), tensor(a1, t, 64), a3[t], a2[t]]) for t in range(4)]


def quad_kernel(g, a1, a3, a2, out3, stats, message3, out_far, stats_far, message):
    q, k, v, do = fours(g, a1, a3, a2)
    ((more, total),) = attend((q, k, v))
    old = [join([stats[i, :64], stats[i, ROWS : ROWS + 64]]) for i in range(2)]
    old = stack([old, unflatten(message3[...])])
    stat, kept, added = combine(old, total, dotted(do, more))
    out_far[...] = join([out3[:64] * kept[:64] + more[:64] * added[:64], out3[64:]])
    stats_far[0], stats_far[1] = stat
    message[...] = flatten(stack([rows_of(stat, 64 * z, 64 * z + 32) for z in range(4)]))


def rest_kernel(
    m0, m1, m2, m3, outs, stats, below, g, a1, a3, a2, out_far, stats_three, stats_far, far5,
    message5, c0, c1, c2, c3,
):
    refs = (m0, m1, m2, m3)
    own = [tensor(g, t) for t in range(4)]
    three = [join([tensor(g, t), tensor(a1, t)]) for t in range(4)]
    four = fours(g, a1, a3, a2)
    five = [
        join([four[t][64 * z : 64 * z + 32] for z in range(4)] + [far5[z, t] for z in range(4)])
        for t in range(4)
    ]
    blocks = []
    for rows, gathered in ((128, three), (64, four), (32, five)):
        mine = [part[:rows] for part in own]
        blocks.append((mine[0], gathered[1], gathered[2], mine[3]))
        blocks.append((gathered[0], mine[1], mine[2], gathered[3]))
    for pair in (0, 2):
        k, v = (join([tensor(refs[pair], t), tensor(refs[pair + 1], t)]) for t in (1, 2))
        q, do = (join([tensor(refs[pair], t, 32), tensor(refs[pair + 1], t, 32)]) for t in (0, 3))
        blocks.append((q, k, v, do))
    k, v = (join([tensor(ref, t, 64) for ref in refs]) for t in (1, 2))
    q, do = (join([tensor(ref, t, 32) for ref in refs]) for t in (0, 3))
    blocks.append((q, k, v, do))
    ((more, total),) = attend(five[:3])
    scores, grads = products(blocks)
    four_stat = [stats_far[0], stats_far[1]]
    three_stat = [stats_three[0], stats_three[1]]
    old = stack(
        [rows_of(four_stat, 64 * z, 64 * z + 32) for z in range(4)] + [unflatten(message5[...])]
    )
    stat5, kept, added = combine(old, total, dotted(five[3], more))
    stat4 = stack(
        [
            rows
            for z in range(4)
            for rows in (
                rows_of(stat5, 32 * z, 32 * z + 32),
                rows_of(four_stat, 64 * z + 32, 64 * z + 64),
            )
        ]
    )
    stat3 = stack(
        [
            rows
            for z in range(2)
            for rows in (
                rows_of(stat4, 64 * z, 64 * z + 64),
                rows_of(three_stat, ROWS * z + 64, ROWS * z + ROWS),
            )
        ]
    )
    own_stat = rows_of(stat3, 0, ROWS)
    out = join([out_far[:32] * kept[:32] + more[:32] * added[:32], out_far[32:]])
    near = group([stats[chip, 0] for chip in range(4)])
    out = out + group([outs[chip] for chip in range(4)]) * jnp.exp(near - own_stat[0])
    stat = [[ungroup(own_stat[i], chip) for i in range(2)] for chip in range(4)]
    block_stats = []
    for rows, gathered in ((128, stat3), (64, stat4), (32, stat5)):
        block_stats += [rows_of(own_stat, 0, rows), gathered]
    block_stats += [stack(stat[:2]), stack(stat[2:]), stack(stat)]
    found = scored(scores, grads, block_stats)
    dqs = [nn(found[i][1], blocks[i][1]) for i in (0, 2, 4, 6, 7, 8)]
    dks = [tn(found[i][1], blocks[i][0]) for i in (1, 3, 5, 6, 7, 8)]
    dvs = [tn(found[i][0], blocks[i][3]) for i in (1, 3, 5, 6, 7, 8)]
    dq, dk, dv = (
        join([f[:32] + g[:32] + h, f[32:64] + g[32:], f[64:]]) for f, g, h, *_ in (dqs, dks, dvs)
    )
    sums = [
        [
            dqs[3 + chip // 2][chip % 2 * 32 : chip % 2 * 32 + 32],
            dks[3 + chip // 2][chip % 2 * ROWS : chip % 2 * ROWS + ROWS],
            dvs[3 + chip // 2][chip % 2 * ROWS : chip % 2 * ROWS + ROWS],
        ]
        for chip in range(4)
    ]
    parts = dqs[5], dks[5], dvs[5]
    for chip, message in enumerate((c0, c1, c2, c3)):
        message[:ROWS] = join([ungroup(out, chip), outs[chip, 32:]]).astype(BF16)
        rows = sums[chip][0] + parts[0][chip * 32 : (chip + 1) * 32] + ungroup(dq, chip)
        message[ROWS : 2 * ROWS] = join([rows, below[chip, 0, 32:]]).astype(BF16)
        for i, top in ((1, dk), (2, dv)):
            whole = below[chip, i] + sums[chip][i]
            part = parts[i][chip * 64 : (chip + 1) * 64]
            rows = join([whole[:32] + part[:32] + ungroup(top, chip), whole[32:64] + part[32:], whole[64:]])
            message[(i + 1) * ROWS : (i + 2) * ROWS] = rows.astype(BF16)
        message[BODY:] = pack(
            [join([stat[chip][i], stats[chip, i, 32:]]) for i in range(2)]
        )


def finish_kernel(steps, q, k, v, do, theirs, places, outs_own, outs_sent, stats_own,
    stats_sent, others, c0, c1, *refs):
    mine_out, theirs_out = refs[-2:]
    messages = (c0, c1)
    tensors = [chip_rows(step, (q, k, v, do), theirs) for step in steps]
    scores, grads = products(tensors)
    terms = [nt(message[BODY:], places[step]) for step, message in zip(steps, messages)]
    finals = [unflatten(rows[:8] + rows[8:16] + rows[16:24]) for rows in terms]
    stat = [[others[step, i] + final[i] for i in range(2)] for step, final in zip(steps, finals)]
    back = [
        nn(places[step], side_by_side([tensor(message, t) for t in range(4)]))
        for step, message in zip(steps, messages)
    ]
    found = scored(scores, grads, stat)
    own = [
        [
            (outs_sent[step - 1] if step else outs_own[0])
            * jnp.exp((stats_sent[step - 1, 0] if step else stats_own[0, 0]) - stat[slot][0])
            for slot, step in enumerate(steps)
        ],
        [nn(score, rows[1]) for (_, score), rows in zip(found, tensors)],
        [tn(score, rows[0]) for (_, score), rows in zip(found, tensors)],
        [tn(chance, rows[3]) for (chance, _), rows in zip(found, tensors)],
    ]
    for slot in range(2):
        for t in range(4):
            rows = own[t][slot] + back[slot][:, t * WIDTH : (t + 1) * WIDTH]
            mine_out[slot, t] = rows[:ROWS].astype(BF16)
            theirs_out[slot, t] = rows[ROWS:].astype(BF16)


def early_kernel(mine0, theirs0, rows):
    for t in range(4):
        for slot in range(2):
            rows[t, :, lanes(own_head(slot))] = mine0[slot, t]
            rows[t, :, lanes(other_head(slot))] = theirs0[slot, t]


def place_kernel(early, mine1, theirs1, att, dq, dk, dv, rows, sems):
    copies = [
        pltpu.make_async_copy(rows.at[t], ref, sems.at[t])
        for t, ref in enumerate((att, dq, dk, dv))
    ]
    for t in range(4):
        rows[t] = early[t]
        for slot in range(2):
            rows[t, :, lanes(own_head(2 + slot))] = mine1[slot, t]
            rows[t, :, lanes(other_head(2 + slot))] = theirs1[slot, t]
        copies[t].start()
    for copy in copies:
        copy.wait()


VMEM = pl.BlockSpec(memory_space=pltpu.VMEM)
LEFT = pl.BlockSpec(memory_space=pltpu.HBM)


def call(kernel, name, outs, *args, left=0, scratch=(), out_specs=None):
    stay = [pltpu.with_memory_space_constraint(arg, pltpu.HBM) for arg in args[:left]]
    args = (*stay, *args[left:])
    return pl.pallas_call(
        kernel,
        name=name,
        out_shape=tuple(jax.ShapeDtypeStruct(shape, dtype) for shape, dtype in outs),
        in_specs=[LEFT] * left + [VMEM] * (len(args) - left),
        out_specs=out_specs or (VMEM,) * len(outs),
        scratch_shapes=scratch,
        compiler_params=pltpu.CompilerParams(vmem_limit_bytes=40 * 2**20),
    )(*args)


def in_plane(array, flip):
    moves = [(PLANE * z + i, PLANE * z + (i ^ flip)) for z in range(DEPTH) for i in range(PLANE)]
    return lax.ppermute(array, "ctx", moves)


def across(array, flip):
    moves = [(PLANE * z + i, PLANE * (z ^ flip) + i) for z in range(DEPTH) for i in range(PLANE)]
    return lax.ppermute(array, "ctx", moves)


def shards(queries, keys, values, out_grad, offsets):
    whole = ((ROWS, HEADS * WIDTH), BF16)
    half = ((CHIPS, 4, ROWS, WIDTH), BF16)
    pairs = ((2, 4, ROWS, WIDTH), BF16)
    message = ((MESSAGE, WIDTH), BF16)
    flat = ((8, WIDTH), F32)
    rows = ((ROWS, WIDTH), F32)
    quads = ((4, ROWS, WIDTH), F32)
    quad_stats = ((4, 2, ROWS, WIDTH), F32)
    chips = ((CHIPS, CHIP, WIDTH), F32)
    chip_stats = ((CHIPS, 2, CHIP, WIDTH), F32)
    seg_stats = ((2, SEG, WIDTH), F32)
    *raw, theirs = call(
        split_kernel, "split", [whole] * 4 + [half], queries, keys, values, out_grad,
        left=4, scratch=[pltpu.SemaphoreType.DMA((4,))],
    )
    theirs = in_plane(theirs, 1)
    picks, places = call(
        maps_kernel, "maps", [((CHIPS, ROWS, CHIP), BF16), ((CHIPS, CHIP, ROWS), BF16)], offsets,
        left=1, scratch=[pltpu.SMEM((6, HEADS), jnp.int32), pltpu.SemaphoreType.DMA((1,))],
    )
    found = []
    for steps in ((1, 2, 3), (0,)):
        sizes = [((len(steps), CHIP, WIDTH), F32), ((len(steps), 2, CHIP, WIDTH), F32)]
        found.append(
            call(
                functools.partial(chip_kernel, steps), "chip", [message] * len(steps) + sizes,
                *raw, theirs, picks,
            )
        )
    (*sent, outs_sent, stats_sent), (kept, outs_own, stats_own) = found
    sent = [kept, *sent]
    (others,) = call(alone_kernel, "alone", [chip_stats], places, stats_own, stats_sent)
    got = [sent[0]] + [in_plane(sent[step], 2 * step) for step in (1, 2, 3)]
    first = call(first_kernel, "first", [((SEG, WIDTH), F32), seg_stats], *got[:2])
    outs, stats, g, g4 = call(
        near_kernel, "near", [quads, quad_stats, message, ((4, 64, WIDTH), BF16)], *got, *first
    )
    (below,) = call(below_kernel, "below", [((4, 3, ROWS, WIDTH), F32)], *got, stats)
    a1 = across(g, 1)
    a3 = across(g4, 3)
    a2 = across(g4, 2)
    out3, stats3, message3 = call(
        pair_kernel, "pair", [rows, seg_stats, flat], g, a1
    )
    a3, a2, message3 = lax.optimization_barrier((a3, a2, across(message3, 3)))
    fars = (g, a1, a3, a2)
    (top,) = call(top_kernel, "top", [((4, 4, 32, WIDTH), BF16)], *fars)
    top = across(top, 6)
    out_far, stats_far, message5 = call(
        quad_kernel, "quad", [rows, seg_stats, flat], *fars, out3, stats3, message3
    )
    message5 = across(message5, 6)
    back = call(
        rest_kernel, "rest", [message] * 4,
        *got, outs, stats, below, *fars, out_far, stats3, stats_far, top, message5,
    )
    back = [back[0]] + [in_plane(back[step], 2 * step) for step in (1, 2, 3)]
    halves, after = [], ()
    for steps in ((0, 1), (2, 3)):
        mine, other = call(
            functools.partial(finish_kernel, steps), "finish", [pairs, pairs],
            *raw, theirs, places, outs_own, outs_sent, stats_own, stats_sent, others, *(back[step] for step in steps), *after,
        )
        after = (mine,)
        halves.append((mine, in_plane(other, 1)))
    (mine0, theirs0), (mine1, theirs1) = halves
    (early,) = call(early_kernel, "early", [((4, ROWS, HEADS * WIDTH), BF16)], mine0, theirs0)
    return call(
        place_kernel, "place", [whole] * 4, early, mine1, theirs1, out_specs=(LEFT,) * 4,
        scratch=[pltpu.VMEM((4, ROWS, HEADS * WIDTH), BF16), pltpu.SemaphoreType.DMA((4,))],
    )


def solution(mesh):
    rows = P(("dp", "ctx"), None)
    return jax.shard_map(
        shards,
        mesh=mesh,
        in_specs=(rows,) * 4 + (P("dp", None),),
        out_specs=(rows,) * 4,
        check_vma=False,
    )
```
